32 devices in a mesh: cable: 2 (over y), chan: 4 (over z), seg: 2 (over x), freq: 2 (over core).
Axes of the slice: x: 2, y: 2, z: 4, core: 2. Of those that a mesh axis runs over, the one named last changes fastest.
Arguments:
- samples: bfloat16 [512, 16, 8192], P(('cable', 'chan'), 'seg'), parts along dimension 0, may hold values from -24 to 24
- live: int32 [512, 16], P('cable'), parts along dimension 0, may hold values from 0 to 1, as said below
Outputs:
- stack: bfloat16 [512, 64, 2, 256], P(('cable', 'chan', 'seg'), None, None, 'freq'), parts along dimension 0
The draws below stay inside these ranges and needn't reach their ends.
There are 2 independent parts, one for each index of `cable`. The reference program is written for one: setup_inputs(seed, part) draws one part's arguments, and reference() takes and returns one part's arrays. A program takes and returns all parts, laid end to end along the dimension named above; each array names one. Nothing has to cross between parts.
Inputs may be any that keep to these rules, and one draw needn't show every extreme that they name: `live`: 1 marks a usable segment of a channel and 0 an unusable one; in every draw some channels are 0 in every segment.
All inputs are finite; a program needn't handle non-finite values.
Results may differ from the reference program's by a relative error of at most 0.006.
Values may be sent and summed in bfloat16 or wider, within the bound.
A program may use at most 64 MiB of HBM per device.

```python
import math
import jax
import jax.numpy as jnp
from jax import lax

CH_DEV = 64
SAMPLES = 8192
BINS = 256
OFFSETS = 64
CHANNELS = 256
SEGMENTS = 16
N_CHAN = 4


def draw_samples(key, part):
    base_key = jax.random.fold_in(key, 101)
    scale_key, noise_key = jax.random.split(base_key, 2)
    spread = jnp.exp(jax.random.uniform(scale_key, (CHANNELS, SEGMENTS), jnp.float32, math.log(0.3), math.log(3.0)))
    noise = jax.random.normal(noise_key, (CHANNELS, SEGMENTS, SAMPLES), jnp.float32)
    values = noise * spread[:, :, None]
    return jnp.clip(values, -24.0, 24.0).astype(jnp.bfloat16)


def draw_live(key, part):
    base_key = jax.random.fold_in(key, 202)
    channel_key, segment_key, forced_key = jax.random.split(base_key, 3)
    dead_channel = jax.random.randint(channel_key, (CHANNELS, 1), 0, 16, dtype=jnp.int32) == 0
    dead_segment = jax.random.randint(segment_key, (CHANNELS, SEGMENTS), 0, 8, dtype=jnp.int32) == 0
    forced = jax.random.randint(forced_key, (), 0, CHANNELS, dtype=jnp.int32)
    forced_dead = jnp.arange(CHANNELS, dtype=jnp.int32)[:, None] == forced
    dead = dead_channel | dead_segment | forced_dead
    return jnp.where(dead, 0, 1).astype(jnp.int32)


def setup_inputs(seed: int = 0, part: int = 0) -> dict:
    arg_keys = jax.random.split(jax.random.key(seed), 3)
    own_keys = jax.random.split(jax.random.fold_in(arg_keys[2], part), 3)
    return {
        "samples": draw_samples(jax.random.fold_in(jax.random.fold_in(arg_keys[2], part), 71), part),
        "live": draw_live(jax.random.fold_in(jax.random.fold_in(arg_keys[2], part), 71), part),
    }


EPSILON = 1e-06

def dft_columns(first_bin, count, length):
    sample_index = jnp.arange(length, dtype=jnp.int32)
    bin_index = first_bin + jnp.arange(count, dtype=jnp.int32)
    phase = sample_index[:, None] * bin_index[None, :] % length
    angle = phase.astype(jnp.float32) * (2.0 * math.pi / length)
    return jnp.concatenate([jnp.cos(angle), -jnp.sin(angle)], axis=1).astype(jnp.bfloat16)

def banded(square, row_count):
    band_width = square.shape[1]
    trailing = square.shape[2:]
    flattened = square.reshape((row_count * band_width,) + trailing)
    padding = jnp.zeros((row_count,) + trailing, square.dtype)
    flattened = jnp.concatenate([flattened, padding], axis=0)
    return flattened.reshape((row_count, band_width + 1) + trailing)[:, :OFFSETS]

def reference(samples, live):
    dft_table = dft_columns(1, BINS, SAMPLES).astype(jnp.float32)
    lag_span = OFFSETS - 1

    def transform(block):
        flat_rows = block.reshape(CH_DEV * SEGMENTS, SAMPLES).astype(jnp.float32)
        spectra = jnp.dot(flat_rows, dft_table, precision=lax.Precision.HIGHEST).reshape(CH_DEV, SEGMENTS, 2, BINS)
        energy = lax.optimization_barrier(jnp.sum(spectra * spectra, axis=(2, 3)))
        scaling = lax.rsqrt(energy / (2 * BINS) + EPSILON)
        return spectra * scaling[:, :, None, None]
    blocks = samples.reshape(N_CHAN, CH_DEV, SEGMENTS, SAMPLES)
    scaled = lax.map(transform, blocks).reshape(CHANNELS, SEGMENTS, 2, BINS)
    whitened = (scaled * live.astype(jnp.float32)[:, :, None, None]).astype(jnp.bfloat16)
    padded = jnp.concatenate([whitened, jnp.zeros((lag_span, SEGMENTS, 2, BINS), jnp.bfloat16)], axis=0)
    live_padded = jnp.concatenate([live, jnp.zeros((lag_span, SEGMENTS), jnp.int32)], axis=0)
    conjugate = jnp.array([1.0, -1.0], jnp.float32).reshape(2, 1)

    def stack_block(first_row):
        window = lax.dynamic_slice_in_dim(padded, first_row, CH_DEV + lag_span, 0).astype(jnp.float32)
        live_rows = lax.dynamic_slice_in_dim(live_padded, first_row, CH_DEV + lag_span, 0).astype(jnp.float32)
        owned = window[:CH_DEV]
        real_part = jnp.einsum('iscf,jscf->ijf', owned, window, precision=lax.Precision.HIGHEST)
        imag_part = jnp.einsum('iscf,jscf->ijf', owned * conjugate, window[:, :, ::-1], precision=lax.Precision.HIGHEST)
        pairs = jnp.dot(live_rows[:CH_DEV], live_rows.T, precision=lax.Precision.HIGHEST)
        numerator = jnp.stack([banded(real_part, CH_DEV), banded(imag_part, CH_DEV)], axis=2)
        return (numerator / jnp.maximum(banded(pairs, CH_DEV), 1.0)[:, :, None, None]).astype(jnp.bfloat16)
    starts = jnp.arange(N_CHAN, dtype=jnp.int32) * CH_DEV
    return lax.map(stack_block, starts).reshape(CHANNELS, OFFSETS, 2, BINS)
```

```python
import functools
import math

import jax
import jax.numpy as jnp
from jax import lax
from jax.experimental import pallas as pl
from jax.experimental.pallas import tpu as pltpu
from jax.sharding import PartitionSpec as P

BINS = 256
OFFSETS = 64
EPSILON = 1e-06
QUARTERS = 4
FINE = 64
CHUNK_CH = 8
KB = 16
MESH = pl.DeviceIdType.MESH


def unit_circle(first, step, count, length):
    t = first + step * lax.broadcasted_iota(jnp.int32, (count, BINS), 0)
    k = 1 + lax.broadcasted_iota(jnp.int32, (count, BINS), 1)
    m = lax.rem(t * k, length)
    m = jnp.where(m >= length // 2, m - length, m)
    y = m.astype(jnp.float32) * (math.pi / length)
    y2 = y * y
    sine = jnp.full_like(y, 1.0 / math.factorial(13))
    for order in (11, 9, 7, 5, 3, 1):
        sine = sine * y2 + (-1.0) ** (order // 2) / math.factorial(order)
    sine = sine * y
    cosine = jnp.full_like(y, -1.0 / math.factorial(14))
    for order in (12, 10, 8, 6, 4, 2, 0):
        cosine = cosine * y2 + (-1.0) ** (order // 2) / math.factorial(order)
    return 1.0 - 2.0 * sine * sine, 2.0 * sine * cosine


def kernel(
    n_chan, n_seg, n_freq, samples, live, out, xs, tab, seeds, snd, win, merged, lv, inv,
    x_sem, send_sem, recv_sem,
):
    length = samples.shape[1]
    quarter = length // QUARTERS
    chans, total_segs = live.shape[0], live.shape[1]
    ch_dev = chans // n_chan
    segs = samples.shape[0] // ch_dev
    owned = ch_dev // n_seg
    half = BINS // n_freq
    core_ch = ch_dev // n_freq
    gpc = n_seg // n_freq
    chunk_rows = CHUNK_CH * segs
    chunks = core_ch // CHUNK_CH
    per_granule = owned // CHUNK_CH
    z, x, c = lax.axis_index("chan"), lax.axis_index("seg"), lax.axis_index("freq")

    def fetch(b, q):
        row = pl.multiple_of((c * chunks + b) * chunk_rows, chunk_rows)
        return pltpu.make_async_copy(
            samples.at[pl.ds(row, chunk_rows), pl.ds(q * quarter, quarter)],
            xs.at[b, pl.ds(q * chunk_rows, chunk_rows), :],
            x_sem.at[b, q],
        )

    for b in range(chunks):
        for q in range(QUARTERS):
            fetch(b, q).start()

    barrier = pltpu.get_barrier_semaphore()
    for dz in (-1, 0, 1):
        near = jnp.logical_and(z + dz >= 0, z + dz < n_chan)
        for tx in range(n_seg):
            for tc in range(n_freq):
                other = near if dz else jnp.logical_or(x != tx, c != tc)

                @pl.when(other)
                def _():
                    pl.semaphore_signal(
                        barrier, inc=1, device_id={"chan": z + dz, "seg": tx, "freq": tc},
                        device_id_type=MESH,
                    )

    fine_cos, fine_sin = unit_circle(0, 1, FINE, length)
    coarse_cos, coarse_sin = unit_circle(0, FINE, quarter // FINE, length)
    seeds[0] = coarse_cos
    seeds[1] = coarse_sin

    def table_rows(a, _):
        ca, sa = seeds[0, pl.ds(a, 1), :], seeds[1, pl.ds(a, 1), :]
        rows = pl.ds(pl.multiple_of(a * FINE, FINE), FINE)
        tab[rows, :BINS] = (ca * fine_cos - sa * fine_sin).astype(jnp.bfloat16)
        tab[rows, BINS:] = (-(sa * fine_cos + ca * fine_sin)).astype(jnp.bfloat16)
        return 0

    lax.fori_loop(0, quarter // FINE, table_rows, 0)

    degree = n_seg * n_freq
    up = (z > 0).astype(jnp.int32)
    down = (z < n_chan - 1).astype(jnp.int32)
    pl.semaphore_wait(barrier, degree - 1 + degree * (up + down))

    def descriptor(b, w, h):
        bb, part = b // per_granule, b % per_granule
        granule = c * gpc + bb
        below = (granule < w).astype(jnp.int32)
        tz, tx = z - below, granule - w + below * n_seg
        rows = pl.ds(pl.multiple_of(b * chunk_rows, chunk_rows), chunk_rows)
        dst_rows = pl.ds(pl.multiple_of(part * chunk_rows, chunk_rows), chunk_rows)
        src = snd.at[h, rows, :]
        dst = win.at[x, w, dst_rows, :]
        remote = pltpu.make_async_remote_copy(
            src_ref=src, dst_ref=dst, send_sem=send_sem.at[b, w, h], recv_sem=recv_sem.at[x, w, part],
            device_id={"chan": tz, "seg": tx, "freq": jnp.int32(h)}, device_id_type=MESH,
        )
        local = pltpu.make_async_copy(src, dst, recv_sem.at[x, w, part])
        mine = jnp.logical_and(jnp.logical_and(tz == z, tx == x), c == h)
        return remote, local, mine, jnp.logical_and(tz >= 0, jnp.logical_not(mine))

    lane_k = 1 + lax.broadcasted_iota(jnp.int32, (1, BINS), 1)
    phase = lane_k % 4
    alpha = jnp.where(phase == 0, 1.0, jnp.where(phase == 2, -1.0, 0.0))
    beta = jnp.where(phase == 1, 1.0, jnp.where(phase == 3, -1.0, 0.0))
    sigma = jnp.where(lane_k % 2 == 0, 1.0, -1.0)

    def transform(b, _):
        for q in range(QUARTERS):
            fetch(b, q).wait()
        acc = jnp.dot(xs[b], tab[...], preferred_element_type=jnp.float32)
        part = [acc[q * chunk_rows : (q + 1) * chunk_rows] for q in range(QUARTERS)]
        re = [p[:, :BINS] for p in part]
        im = [p[:, BINS:] for p in part]
        odd_re, odd_im = re[1] + sigma * re[3], im[1] + sigma * im[3]
        full_re = re[0] + sigma * re[2] + (alpha * odd_re + beta * odd_im)
        full_im = im[0] + sigma * im[2] + (alpha * odd_im - beta * odd_re)
        energy = jnp.sum(full_re * full_re + full_im * full_im, axis=1, keepdims=True)
        scaling = lax.rsqrt(energy / (2 * BINS) + EPSILON)
        first = pl.multiple_of(z * ch_dev + c * core_ch + b * CHUNK_CH, CHUNK_CH)
        usable = live[pl.ds(first, CHUNK_CH), :].astype(jnp.float32)
        usable = jnp.broadcast_to(usable[:, None, :], (CHUNK_CH, segs, total_segs))
        column = lax.broadcasted_iota(jnp.int32, usable.shape, 2)
        segment = x * segs + lax.broadcasted_iota(jnp.int32, usable.shape, 1)
        usable = jnp.where(column == segment, usable, 0.0).reshape(chunk_rows, total_segs)
        usable = jnp.sum(usable, axis=1, keepdims=True)
        white_re = (full_re * scaling * usable).astype(jnp.bfloat16)
        white_im = (full_im * scaling * usable).astype(jnp.bfloat16)
        rows = pl.ds(pl.multiple_of(b * chunk_rows, chunk_rows), chunk_rows)
        for h in range(n_freq):
            snd[h, rows, :half] = white_re[:, h * half : (h + 1) * half]
            snd[h, rows, half:] = white_im[:, h * half : (h + 1) * half]
        for w in range(n_seg, -1, -1):
            for h in range(n_freq):
                remote, local, mine, other = descriptor(b, w, h)
                pl.when(other)(remote.start)
                pl.when(mine)(local.start)
        return 0

    lax.fori_loop(0, chunks, transform, 0)

    last_block = chans // owned - 1
    for w in range(n_seg + 1):
        block = z * n_seg + x + w
        row = pl.multiple_of(jnp.minimum(block, last_block) * owned, owned)
        rows = live[pl.ds(row, owned), :].astype(jnp.float32)
        lv[w * owned : (w + 1) * owned, :] = jnp.where(block <= last_block, rows, 0.0)
    twice = (
        lax.broadcasted_iota(jnp.int32, (2 * OFFSETS, OFFSETS), 0) // 2
        == lax.broadcasted_iota(jnp.int32, (2 * OFFSETS, OFFSETS), 1)
    ).astype(jnp.float32).astype(jnp.bfloat16)
    ones = jnp.ones((total_segs, half), jnp.bfloat16)

    def count_pairs(i, _):
        both = (lv[pl.ds(i, OFFSETS), :] * lv[pl.ds(i, 1), :]).astype(jnp.bfloat16)
        both = jnp.dot(twice, both, preferred_element_type=jnp.float32).astype(jnp.bfloat16)
        pairs = jnp.dot(both, ones, preferred_element_type=jnp.float32)
        inv[i] = 1.0 / jnp.maximum(pairs, 1.0)
        return 0

    lax.fori_loop(0, owned, count_pairs, 0, unroll=4)

    span = n_seg * segs
    row_id = lax.broadcasted_iota(jnp.int32, (2 * KB, KB * span), 0)
    col_id = lax.broadcasted_iota(jnp.int32, (2 * KB, KB * span), 1) // span
    hit = row_id // 2 == col_id
    sum_re = jnp.where(jnp.logical_and(hit, row_id % 2 == 0), 1.0, 0.0).astype(jnp.bfloat16)
    sum_im = jnp.where(jnp.logical_and(hit, row_id % 2 == 1), 1.0, 0.0).astype(jnp.bfloat16)

    for w in range(n_seg + 1):
        inside = z + (x + w) // n_seg < n_chan

        @pl.when(inside)
        def _():
            for sx in range(n_seg):
                for part in range(per_granule):
                    rows = pl.ds(part * chunk_rows, chunk_rows)
                    dst = win.at[sx, w, rows, :]
                    pltpu.make_async_copy(dst, dst, recv_sem.at[sx, w, part]).wait()

            def merge(m, _):
                rows = pl.ds(pl.multiple_of(m * 2 * segs, 2 * segs), 2 * segs)
                parts = [win[sx, w, rows, :].astype(jnp.float32) for sx in range(n_seg)]
                for e in range(2):
                    whole = jnp.concatenate([p[e * segs : (e + 1) * segs] for p in parts], axis=0)
                    merged[w * owned + 2 * m + e] = whole.astype(jnp.bfloat16)
                return 0

            lax.fori_loop(0, owned // 2, merge, 0, unroll=4)

        @pl.when(jnp.logical_not(inside))
        def _():
            zeros = jnp.zeros((owned,) + merged.shape[1:], jnp.bfloat16)
            merged[w * owned : (w + 1) * owned] = zeros

        for kb in range(OFFSETS // KB):
            low = max(0, owned * w - KB * kb - KB + 1)
            high = min(owned, owned * (w + 1) - KB * kb - KB + 1)

            def correlate(i, _):
                own = merged[i]
                other = merged[pl.ds(i + KB * kb, KB)]
                own_re, own_im = own[None, :, :half], own[None, :, half:]
                other_re, other_im = other[:, :, :half], other[:, :, half:]
                re = own_re * other_re + own_im * other_im
                im = own_re * other_im - own_im * other_re
                total = jnp.dot(
                    sum_re, re.reshape(KB * span, half), preferred_element_type=jnp.float32
                ) + jnp.dot(sum_im, im.reshape(KB * span, half), preferred_element_type=jnp.float32)
                rows = pl.ds(2 * KB * kb, 2 * KB)
                out[i, rows, :] = (total * inv[i, rows, :]).astype(jnp.bfloat16)
                return 0

            if low < high:
                lax.fori_loop(low, high, correlate, 0, unroll=min(8, high - low))

    def drain(b, _):
        for w in range(n_seg + 1):
            for h in range(n_freq):
                remote, local, mine, other = descriptor(b, w, h)
                pl.when(other)(remote.wait_send)
        return 0

    lax.fori_loop(0, chunks, drain, 0)


def shards(samples, live):
    ch_dev, segs, length = samples.shape
    n_chan, n_seg, n_freq = (lax.axis_size(a) for a in ("chan", "seg", "freq"))
    owned = ch_dev // n_seg
    half = BINS // n_freq
    core_ch = ch_dev // n_freq
    chunks = core_ch // CHUNK_CH
    chunk_rows = CHUNK_CH * segs
    quarter = length // QUARTERS
    window = (n_seg + 1) * owned
    result = pl.pallas_call(
        functools.partial(kernel, n_chan, n_seg, n_freq),
        out_shape=jax.ShapeDtypeStruct((owned, 2 * OFFSETS, half), jnp.bfloat16),
        in_specs=[pl.BlockSpec(memory_space=pl.ANY), pl.BlockSpec(memory_space=pltpu.VMEM)],
        out_specs=pl.BlockSpec(memory_space=pltpu.VMEM),
        scratch_shapes=[
            pltpu.VMEM((chunks, QUARTERS * chunk_rows, quarter), jnp.bfloat16),
            pltpu.VMEM((quarter, 2 * BINS), jnp.bfloat16),
            pltpu.VMEM((2, quarter // FINE, BINS), jnp.float32),
            pltpu.VMEM((n_freq, core_ch * segs, 2 * half), jnp.bfloat16),
            pltpu.VMEM((n_seg, n_seg + 1, owned * segs, 2 * half), jnp.bfloat16),
            pltpu.VMEM((window, n_seg * segs, 2 * half), jnp.bfloat16),
            pltpu.VMEM((window, n_seg * segs), jnp.float32),
            pltpu.VMEM((owned, 2 * OFFSETS, half), jnp.float32),
            pltpu.SemaphoreType.DMA((chunks, QUARTERS)),
            pltpu.SemaphoreType.DMA((chunks, n_seg + 1, n_freq)),
            pltpu.SemaphoreType.DMA((n_seg, n_seg + 1, owned // CHUNK_CH)),
        ],
        compiler_params=pltpu.CompilerParams(
            collective_id=0, has_side_effects=True, vmem_limit_bytes=48 * 1024 * 1024
        ),
    )(samples.reshape(ch_dev * segs, length), live)
    return result.reshape(owned, OFFSETS, 2, half)


def solution(mesh):
    return jax.shard_map(
        shards,
        mesh=mesh,
        in_specs=(P(("cable", "chan"), "seg", None), P("cable", None)),
        out_specs=P(("cable", "chan", "seg"), None, None, "freq"),
        check_vma=False,
    )
```

```python
import functools
import math

import jax
import jax.numpy as jnp
from jax import lax
from jax.experimental import pallas as pl
from jax.experimental.pallas import tpu as pltpu
from jax.sharding import PartitionSpec as P

BINS = 256
OFFSETS = 64
EPSILON = 1e-06
QUARTERS = 4
FINE = 64
CHUNK_CH = 8
KB = 16
MESH = pl.DeviceIdType.MESH


def unit_circle(first, step, count, length):
    t = first + step * lax.broadcasted_iota(jnp.int32, (count, BINS), 0)
    k = 1 + lax.broadcasted_iota(jnp.int32, (count, BINS), 1)
    m = lax.rem(t * k, length)
    m = jnp.where(m >= length // 2, m - length, m)
    y = m.astype(jnp.float32) * (math.pi / length)
    y2 = y * y
    sine = jnp.full_like(y, 1.0 / math.factorial(13))
    for order in (11, 9, 7, 5, 3, 1):
        sine = sine * y2 + (-1.0) ** (order // 2) / math.factorial(order)
    sine = sine * y
    cosine = jnp.full_like(y, -1.0 / math.factorial(14))
    for order in (12, 10, 8, 6, 4, 2, 0):
        cosine = cosine * y2 + (-1.0) ** (order // 2) / math.factorial(order)
    return 1.0 - 2.0 * sine * sine, 2.0 * sine * cosine


def kernel(
    n_chan, n_seg, n_freq, samples, live_hbm, out, live_in, live, xs, tab, seeds, snd, win, merged, lv, inv,
    live_sem, x_sem, send_sem, recv_sem, along_sem, across_sem,
):
    length = samples.shape[1]
    quarter = length // QUARTERS
    total_segs, chans = live_in.shape
    ch_dev = chans // n_chan
    segs = samples.shape[0] // ch_dev
    owned = ch_dev // n_seg
    half = BINS // n_freq
    core_ch = ch_dev // n_freq
    gpc = n_seg // n_freq
    chunk_rows = CHUNK_CH * segs
    chunks = core_ch // CHUNK_CH
    per_granule = owned // CHUNK_CH
    z, x, c = lax.axis_index("chan"), lax.axis_index("seg"), lax.axis_index("freq")

    def fetch(b, q):
        row = pl.multiple_of((c * chunks + b) * chunk_rows, chunk_rows)
        return pltpu.make_async_copy(
            samples.at[pl.ds(row, chunk_rows), pl.ds(q * quarter, quarter)],
            xs.at[b, pl.ds(q * chunk_rows, chunk_rows), :],
            x_sem.at[b, q],
        )

    for b in range(chunks):
        for q in range(QUARTERS):
            fetch(b, q).start()
    live_copy = pltpu.make_async_copy(live_hbm, live_in, live_sem)
    live_copy.start()

    barrier = pltpu.get_barrier_semaphore()
    for dz in (-1, 0, 1):
        near = jnp.logical_and(z + dz >= 0, z + dz < n_chan)
        for tx in range(n_seg):
            for tc in range(n_freq):
                other = near if dz else jnp.logical_or(x != tx, c != tc)

                @pl.when(other)
                def _():
                    pl.semaphore_signal(
                        barrier, inc=1, device_id={"chan": z + dz, "seg": tx, "freq": tc},
                        device_id_type=MESH,
                    )

    fine_cos, fine_sin = unit_circle(0, 1, FINE, length)
    coarse_cos, coarse_sin = unit_circle(0, FINE, quarter // FINE, length)
    seeds[0] = coarse_cos
    seeds[1] = coarse_sin

    def table_rows(a, _):
        ca, sa = seeds[0, pl.ds(a, 1), :], seeds[1, pl.ds(a, 1), :]
        rows = pl.ds(pl.multiple_of(a * FINE, FINE), FINE)
        tab[rows, :BINS] = (ca * fine_cos - sa * fine_sin).astype(jnp.bfloat16)
        tab[rows, BINS:] = (-(sa * fine_cos + ca * fine_sin)).astype(jnp.bfloat16)
        return 0

    lax.fori_loop(0, quarter // FINE, table_rows, 0)

    live_copy.wait()
    live[...] = live_in[...].astype(jnp.float32).T
    degree = n_seg * n_freq
    up = (z > 0).astype(jnp.int32)
    down = (z < n_chan - 1).astype(jnp.int32)
    pl.semaphore_wait(barrier, degree - 1 + degree * (up + down))

    def descriptor(b, w, h):
        bb, part = b // per_granule, b % per_granule
        granule = c * gpc + bb
        below = (granule < w).astype(jnp.int32)
        tz, tx = z - below, granule - w + below * n_seg
        rows = pl.ds(pl.multiple_of(b * chunk_rows, chunk_rows), chunk_rows)
        dst_rows = pl.ds(pl.multiple_of(part * chunk_rows, chunk_rows), chunk_rows)
        src = snd.at[h, rows, :]
        dst = win.at[x, w, dst_rows, :]
        remote = pltpu.make_async_remote_copy(
            src_ref=src, dst_ref=dst, send_sem=send_sem.at[b, w, h], recv_sem=recv_sem.at[x, w, part],
            device_id={"chan": tz, "seg": tx, "freq": jnp.int32(h)}, device_id_type=MESH,
        )
        local = pltpu.make_async_copy(src, dst, recv_sem.at[x, w, part])
        mine = jnp.logical_and(jnp.logical_and(tz == z, tx == x), c == h)
        straight = jnp.logical_or(below == 0, jnp.logical_and(tz >= 0, tx == x))
        return remote, local, mine, jnp.logical_and(straight, jnp.logical_not(mine))

    def arrived(sx, w, part):
        dst = win.at[sx, w, pl.ds(part * chunk_rows, chunk_rows), :]
        pltpu.make_async_copy(dst, dst, recv_sem.at[sx, w, part]).wait()

    def relay(sx, w, part, to_w, tz, tx, sem):
        rows = pl.ds(part * chunk_rows, chunk_rows)
        return pltpu.make_async_remote_copy(
            src_ref=win.at[sx, w, rows, :], dst_ref=win.at[sx, to_w, rows, :], send_sem=sem,
            recv_sem=recv_sem.at[sx, to_w, part],
            device_id={"chan": tz, "seg": tx, "freq": c}, device_id_type=MESH,
        )

    def along(sx, part):
        return relay(sx, 0, part, n_seg, z - 1, x, along_sem.at[sx, part])

    def across(sx, w, tx, part):
        return relay(sx, w, part, w + x - tx, z, jnp.int32(tx), across_sem.at[sx, w - 1, tx, part])

    has_above = z < n_chan - 1

    def is_hub(sx, w):
        granule = x + w - n_seg
        own = jnp.logical_and(sx == x, jnp.logical_and(granule >= 0, granule < n_seg - 1))
        own = jnp.logical_and(own, jnp.logical_or(granule < n_seg - 2, x < n_seg - 1))
        first = jnp.logical_and(w == n_seg, jnp.logical_and(sx < x, x < n_seg - 1))
        return jnp.logical_and(has_above, jnp.logical_or(own, first))

    def hub_target(sx, w, tx):
        return jnp.logical_and(is_hub(sx, w), jnp.logical_and(tx > x + w - n_seg, tx != x))

    lane_k = 1 + lax.broadcasted_iota(jnp.int32, (1, BINS), 1)
    phase = lane_k % 4
    alpha = jnp.where(phase == 0, 1.0, jnp.where(phase == 2, -1.0, 0.0))
    beta = jnp.where(phase == 1, 1.0, jnp.where(phase == 3, -1.0, 0.0))
    sigma = jnp.where(lane_k % 2 == 0, 1.0, -1.0)

    def transform(b, _):
        for q in range(QUARTERS):
            fetch(b, q).wait()
        acc = jnp.dot(xs[b], tab[...], preferred_element_type=jnp.float32)
        part = [acc[q * chunk_rows : (q + 1) * chunk_rows] for q in range(QUARTERS)]
        re = [p[:, :BINS] for p in part]
        im = [p[:, BINS:] for p in part]
        odd_re, odd_im = re[1] + sigma * re[3], im[1] + sigma * im[3]
        full_re = re[0] + sigma * re[2] + (alpha * odd_re + beta * odd_im)
        full_im = im[0] + sigma * im[2] + (alpha * odd_im - beta * odd_re)
        energy = jnp.sum(full_re * full_re + full_im * full_im, axis=1, keepdims=True)
        scaling = lax.rsqrt(energy / (2 * BINS) + EPSILON)
        first = pl.multiple_of(z * ch_dev + c * core_ch + b * CHUNK_CH, CHUNK_CH)
        usable = live[pl.ds(first, CHUNK_CH), :]
        usable = jnp.broadcast_to(usable[:, None, :], (CHUNK_CH, segs, total_segs))
        column = lax.broadcasted_iota(jnp.int32, usable.shape, 2)
        segment = x * segs + lax.broadcasted_iota(jnp.int32, usable.shape, 1)
        usable = jnp.where(column == segment, usable, 0.0).reshape(chunk_rows, total_segs)
        usable = jnp.sum(usable, axis=1, keepdims=True)
        white_re = (full_re * scaling * usable).astype(jnp.bfloat16)
        white_im = (full_im * scaling * usable).astype(jnp.bfloat16)
        rows = pl.ds(pl.multiple_of(b * chunk_rows, chunk_rows), chunk_rows)
        for h in range(n_freq):
            snd[h, rows, :half] = white_re[:, h * half : (h + 1) * half]
            snd[h, rows, half:] = white_im[:, h * half : (h + 1) * half]
        for w in range(n_seg, -1, -1):
            for h in range(n_freq):
                remote, local, mine, other = descriptor(b, w, h)
                pl.when(other)(remote.start)
                pl.when(mine)(local.start)
        return 0

    lax.fori_loop(0, chunks, transform, 0)

    for part in range(per_granule):
        for sx in range(n_seg):
            arrived(sx, 0, part)

            @pl.when(jnp.logical_and(z > 0, sx != x))
            def _():
                along(sx, part).start()

    for w in range(n_seg, 0, -1):
        for sx in range(n_seg):

            @pl.when(is_hub(sx, w))
            def _():
                for part in range(per_granule):
                    arrived(sx, w, part)
                    for tx in range(n_seg):
                        pl.when(hub_target(sx, w, tx))(across(sx, w, tx, part).start)

    last_block = chans // owned - 1
    for w in range(n_seg + 1):
        block = z * n_seg + x + w
        row = pl.multiple_of(jnp.minimum(block, last_block) * owned, owned)
        rows = live[pl.ds(row, owned), :]
        lv[w * owned : (w + 1) * owned, :] = jnp.where(block <= last_block, rows, 0.0)
    twice = (
        lax.broadcasted_iota(jnp.int32, (2 * OFFSETS, OFFSETS), 0) // 2
        == lax.broadcasted_iota(jnp.int32, (2 * OFFSETS, OFFSETS), 1)
    ).astype(jnp.float32).astype(jnp.bfloat16)
    ones = jnp.ones((total_segs, half), jnp.bfloat16)

    def count_pairs(i, _):
        both = (lv[pl.ds(i, OFFSETS), :] * lv[pl.ds(i, 1), :]).astype(jnp.bfloat16)
        both = jnp.dot(twice, both, preferred_element_type=jnp.float32).astype(jnp.bfloat16)
        pairs = jnp.dot(both, ones, preferred_element_type=jnp.float32)
        inv[i] = 1.0 / jnp.maximum(pairs, 1.0)
        return 0

    lax.fori_loop(0, owned, count_pairs, 0, unroll=4)

    span = n_seg * segs
    row_id = lax.broadcasted_iota(jnp.int32, (2 * KB, KB * span), 0)
    col_id = lax.broadcasted_iota(jnp.int32, (2 * KB, KB * span), 1) // span
    hit = row_id // 2 == col_id
    sum_re = jnp.where(jnp.logical_and(hit, row_id % 2 == 0), 1.0, 0.0).astype(jnp.bfloat16)
    sum_im = jnp.where(jnp.logical_and(hit, row_id % 2 == 1), 1.0, 0.0).astype(jnp.bfloat16)

    for w in range(n_seg + 1):
        inside = z + (x + w) // n_seg < n_chan

        @pl.when(inside)
        def _():
            for sx in range(n_seg):
                if w > 0:

                    @pl.when(jnp.logical_not(is_hub(sx, w)))
                    def _():
                        for part in range(per_granule):
                            arrived(sx, w, part)

            def merge(m, _):
                rows = pl.ds(pl.multiple_of(m * 2 * segs, 2 * segs), 2 * segs)
                parts = [win[sx, w, rows, :].astype(jnp.float32) for sx in range(n_seg)]
                for e in range(2):
                    whole = jnp.concatenate([p[e * segs : (e + 1) * segs] for p in parts], axis=0)
                    merged[w * owned + 2 * m + e] = whole.astype(jnp.bfloat16)
                return 0

            lax.fori_loop(0, owned // 2, merge, 0, unroll=4)

        @pl.when(jnp.logical_not(inside))
        def _():
            zeros = jnp.zeros((owned,) + merged.shape[1:], jnp.bfloat16)
            merged[w * owned : (w + 1) * owned] = zeros

        for kb in range(OFFSETS // KB):
            low = max(0, owned * w - KB * kb - KB + 1)
            high = min(owned, owned * (w + 1) - KB * kb - KB + 1)

            def correlate(i, _):
                own = merged[i]
                other = merged[pl.ds(i + KB * kb, KB)]
                own_re, own_im = own[None, :, :half], own[None, :, half:]
                other_re, other_im = other[:, :, :half], other[:, :, half:]
                re = own_re * other_re + own_im * other_im
                im = own_re * other_im - own_im * other_re
                total = jnp.dot(
                    sum_re, re.reshape(KB * span, half), preferred_element_type=jnp.float32
                ) + jnp.dot(sum_im, im.reshape(KB * span, half), preferred_element_type=jnp.float32)
                rows = pl.ds(2 * KB * kb, 2 * KB)
                out[i, rows, :] = (total * inv[i, rows, :]).astype(jnp.bfloat16)
                return 0

            if low < high:
                lax.fori_loop(low, high, correlate, 0, unroll=min(8, high - low))

    def drain(b, _):
        for w in range(n_seg + 1):
            for h in range(n_freq):
                remote, local, mine, other = descriptor(b, w, h)
                pl.when(other)(remote.wait_send)
        return 0

    lax.fori_loop(0, chunks, drain, 0)
    for part in range(per_granule):
        for sx in range(n_seg):
            pl.when(jnp.logical_and(z > 0, sx != x))(along(sx, part).wait_send)
            for w in range(1, n_seg + 1):
                for tx in range(n_seg):
                    pl.when(hub_target(sx, w, tx))(across(sx, w, tx, part).wait_send)


def shards(samples, live):
    ch_dev, segs, length = samples.shape
    n_chan, n_seg, n_freq = (lax.axis_size(a) for a in ("chan", "seg", "freq"))
    owned = ch_dev // n_seg
    half = BINS // n_freq
    core_ch = ch_dev // n_freq
    chunks = core_ch // CHUNK_CH
    chunk_rows = CHUNK_CH * segs
    quarter = length // QUARTERS
    window = (n_seg + 1) * owned
    result = pl.pallas_call(
        functools.partial(kernel, n_chan, n_seg, n_freq),
        out_shape=jax.ShapeDtypeStruct((owned, 2 * OFFSETS, half), jnp.bfloat16),
        in_specs=[pl.BlockSpec(memory_space=pl.ANY)] * 2,
        out_specs=pl.BlockSpec(memory_space=pltpu.VMEM),
        scratch_shapes=[
            pltpu.VMEM(live.shape[::-1], jnp.int32),
            pltpu.VMEM(live.shape, jnp.float32),
            pltpu.VMEM((chunks, QUARTERS * chunk_rows, quarter), jnp.bfloat16),
            pltpu.VMEM((quarter, 2 * BINS), jnp.bfloat16),
            pltpu.VMEM((2, quarter // FINE, BINS), jnp.float32),
            pltpu.VMEM((n_freq, core_ch * segs, 2 * half), jnp.bfloat16),
            pltpu.VMEM((n_seg, n_seg + 1, owned * segs, 2 * half), jnp.bfloat16),
            pltpu.VMEM((window, n_seg * segs, 2 * half), jnp.bfloat16),
            pltpu.VMEM((window, n_seg * segs), jnp.float32),
            pltpu.VMEM((owned, 2 * OFFSETS, half), jnp.float32),
            pltpu.SemaphoreType.DMA,
            pltpu.SemaphoreType.DMA((chunks, QUARTERS)),
            pltpu.SemaphoreType.DMA((chunks, n_seg + 1, n_freq)),
            pltpu.SemaphoreType.DMA((n_seg, n_seg + 1, owned // CHUNK_CH)),
            pltpu.SemaphoreType.DMA((n_seg, owned // CHUNK_CH)),
            pltpu.SemaphoreType.DMA((n_seg, n_seg, n_seg, owned // CHUNK_CH)),
        ],
        compiler_params=pltpu.CompilerParams(
            collective_id=0, has_side_effects=True, vmem_limit_bytes=48 * 1024 * 1024
        ),
    )(samples.reshape(ch_dev * segs, length), live.T)
    return result.reshape(owned, OFFSETS, 2, half)


def solution(mesh):
    return jax.shard_map(
        shards,
        mesh=mesh,
        in_specs=(P(("cable", "chan"), "seg", None), P("cable", None)),
        out_specs=P(("cable", "chan", "seg"), None, None, "freq"),
        check_vma=False,
    )
```

```python
import functools
import math

import jax
import jax.numpy as jnp
from jax import lax
from jax.experimental import pallas as pl
from jax.experimental.pallas import tpu as pltpu
from jax.sharding import PartitionSpec as P

BINS = 256
OFFSETS = 64
EPSILON = 1e-06
QUARTERS = 4
FINE = 64
CHUNK_CH = 8
KB = 16
MESH = pl.DeviceIdType.MESH


def unit_circle(first, step, count, length):
    t = first + step * lax.broadcasted_iota(jnp.int32, (count, BINS), 0)
    k = 1 + lax.broadcasted_iota(jnp.int32, (count, BINS), 1)
    m = lax.rem(t * k, length)
    m = jnp.where(m >= length // 2, m - length, m)
    y = m.astype(jnp.float32) * (math.pi / length)
    y2 = y * y
    sine = jnp.full_like(y, 1.0 / math.factorial(13))
    for order in (11, 9, 7, 5, 3, 1):
        sine = sine * y2 + (-1.0) ** (order // 2) / math.factorial(order)
    sine = sine * y
    cosine = jnp.full_like(y, -1.0 / math.factorial(14))
    for order in (12, 10, 8, 6, 4, 2, 0):
        cosine = cosine * y2 + (-1.0) ** (order // 2) / math.factorial(order)
    return 1.0 - 2.0 * sine * sine, 2.0 * sine * cosine


def kernel(
    n_chan, n_seg, n_freq, samples, live_hbm, out, live_in, live, xs, tab, seeds, snd, win, merged, lv, inv,
    live_sem, x_sem, send_sem, recv_sem, along_sem, across_sem,
):
    length = samples.shape[1]
    quarter = length // QUARTERS
    total_segs, chans = live_in.shape
    ch_dev = chans // n_chan
    segs = samples.shape[0] // ch_dev
    owned = ch_dev // n_seg
    half = BINS // n_freq
    core_ch = ch_dev // n_freq
    gpc = n_seg // n_freq
    chunk_rows = CHUNK_CH * segs
    chunks = core_ch // CHUNK_CH
    per_granule = owned // CHUNK_CH
    z, x, c = lax.axis_index("chan"), lax.axis_index("seg"), lax.axis_index("freq")

    def fetch(b, q):
        row = pl.multiple_of((c * chunks + b) * chunk_rows, chunk_rows)
        return pltpu.make_async_copy(
            samples.at[pl.ds(row, chunk_rows), pl.ds(q * quarter, quarter)],
            xs.at[b, pl.ds(q * chunk_rows, chunk_rows), :],
            x_sem.at[b, q],
        )

    for b in range(chunks):
        for q in range(QUARTERS):
            fetch(b, q).start()
    live_copy = pltpu.make_async_copy(live_hbm, live_in, live_sem)
    live_copy.start()

    barrier = pltpu.get_barrier_semaphore()
    for dz in (-1, 0, 1):
        near = jnp.logical_and(z + dz >= 0, z + dz < n_chan)
        for tx in range(n_seg):
            for tc in range(n_freq):
                other = near if dz else jnp.logical_or(x != tx, c != tc)

                @pl.when(other)
                def _():
                    pl.semaphore_signal(
                        barrier, inc=1, device_id={"chan": z + dz, "seg": tx, "freq": tc},
                        device_id_type=MESH,
                    )

    fine_cos, fine_sin = unit_circle(0, 1, FINE, length)
    coarse_cos, coarse_sin = unit_circle(0, FINE, quarter // FINE, length)
    seeds[0] = coarse_cos
    seeds[1] = coarse_sin

    def table_rows(a, _):
        ca, sa = seeds[0, pl.ds(a, 1), :], seeds[1, pl.ds(a, 1), :]
        rows = pl.ds(pl.multiple_of(a * FINE, FINE), FINE)
        tab[rows, :BINS] = (ca * fine_cos - sa * fine_sin).astype(jnp.bfloat16)
        tab[rows, BINS:] = (-(sa * fine_cos + ca * fine_sin)).astype(jnp.bfloat16)
        return 0

    lax.fori_loop(0, quarter // FINE, table_rows, 0)

    live_copy.wait()
    live[...] = live_in[...].astype(jnp.float32).T
    degree = n_seg * n_freq
    up = (z > 0).astype(jnp.int32)
    down = (z < n_chan - 1).astype(jnp.int32)
    pl.semaphore_wait(barrier, degree - 1 + degree * (up + down))

    def descriptor(b, w, h):
        bb, part = b // per_granule, b % per_granule
        granule = c * gpc + bb
        below = (granule < w).astype(jnp.int32)
        tz, tx = z - below, granule - w + below * n_seg
        rows = pl.ds(pl.multiple_of(b * chunk_rows, chunk_rows), chunk_rows)
        dst_rows = pl.ds(pl.multiple_of(part * chunk_rows, chunk_rows), chunk_rows)
        src = snd.at[h, rows, :]
        dst = win.at[x, w, dst_rows, :]
        remote = pltpu.make_async_remote_copy(
            src_ref=src, dst_ref=dst, send_sem=send_sem.at[b, w, h], recv_sem=recv_sem.at[x, w, part],
            device_id={"chan": tz, "seg": tx, "freq": jnp.int32(h)}, device_id_type=MESH,
        )
        local = pltpu.make_async_copy(src, dst, recv_sem.at[x, w, part])
        mine = jnp.logical_and(jnp.logical_and(tz == z, tx == x), c == h)
        straight = jnp.logical_or(below == 0, jnp.logical_and(tz >= 0, tx == x))
        return remote, local, mine, jnp.logical_and(straight, jnp.logical_not(mine))

    def arrived(sx, w, part):
        dst = win.at[sx, w, pl.ds(part * chunk_rows, chunk_rows), :]
        pltpu.make_async_copy(dst, dst, recv_sem.at[sx, w, part]).wait()

    def relay(sx, w, part, to_w, tz, tx, sem):
        rows = pl.ds(part * chunk_rows, chunk_rows)
        return pltpu.make_async_remote_copy(
            src_ref=win.at[sx, w, rows, :], dst_ref=win.at[sx, to_w, rows, :], send_sem=sem,
            recv_sem=recv_sem.at[sx, to_w, part],
            device_id={"chan": tz, "seg": tx, "freq": c}, device_id_type=MESH,
        )

    def along(sx, part):
        return relay(sx, 0, part, n_seg, z - 1, x, along_sem.at[sx, part])

    def across(sx, w, tx, part):
        return relay(sx, w, part, w + x - tx, z, jnp.int32(tx), across_sem.at[sx, w - 1, tx, part])

    has_above = z < n_chan - 1

    def is_hub(sx, w):
        granule = x + w - n_seg
        own = jnp.logical_and(sx == x, jnp.logical_and(granule >= 0, granule < n_seg - 1))
        own = jnp.logical_and(own, jnp.logical_or(granule < n_seg - 2, x < n_seg - 1))
        first = jnp.logical_and(w == n_seg, jnp.logical_and(sx < x, x < n_seg - 1))
        return jnp.logical_and(has_above, jnp.logical_or(own, first))

    def hub_target(sx, w, tx):
        return jnp.logical_and(is_hub(sx, w), jnp.logical_and(tx > x + w - n_seg, tx != x))

    lane_k = 1 + lax.broadcasted_iota(jnp.int32, (1, BINS), 1)
    phase = lane_k % 4
    alpha = jnp.where(phase == 0, 1.0, jnp.where(phase == 2, -1.0, 0.0))
    beta = jnp.where(phase == 1, 1.0, jnp.where(phase == 3, -1.0, 0.0))
    sigma = jnp.where(lane_k % 2 == 0, 1.0, -1.0)

    def transform(b, _):
        for q in range(QUARTERS):
            fetch(b, q).wait()
        acc = jnp.dot(xs[b], tab[...], preferred_element_type=jnp.float32)
        part = [acc[q * chunk_rows : (q + 1) * chunk_rows] for q in range(QUARTERS)]
        re = [p[:, :BINS] for p in part]
        im = [p[:, BINS:] for p in part]
        odd_re, odd_im = re[1] + sigma * re[3], im[1] + sigma * im[3]
        full_re = re[0] + sigma * re[2] + (alpha * odd_re + beta * odd_im)
        full_im = im[0] + sigma * im[2] + (alpha * odd_im - beta * odd_re)
        energy = jnp.sum(full_re * full_re + full_im * full_im, axis=1, keepdims=True)
        scaling = lax.rsqrt(energy / (2 * BINS) + EPSILON)
        first = pl.multiple_of(z * ch_dev + c * core_ch + b * CHUNK_CH, CHUNK_CH)
        usable = live[pl.ds(first, CHUNK_CH), :]
        usable = jnp.broadcast_to(usable[:, None, :], (CHUNK_CH, segs, total_segs))
        column = lax.broadcasted_iota(jnp.int32, usable.shape, 2)
        segment = x * segs + lax.broadcasted_iota(jnp.int32, usable.shape, 1)
        usable = jnp.where(column == segment, usable, 0.0).reshape(chunk_rows, total_segs)
        usable = jnp.sum(usable, axis=1, keepdims=True)
        white_re = (full_re * scaling * usable).astype(jnp.bfloat16)
        white_im = (full_im * scaling * usable).astype(jnp.bfloat16)
        rows = pl.ds(pl.multiple_of(b * chunk_rows, chunk_rows), chunk_rows)
        for h in range(n_freq):
            snd[h, rows, :half] = white_re[:, h * half : (h + 1) * half]
            snd[h, rows, half:] = white_im[:, h * half : (h + 1) * half]
        for w in range(n_seg, -1, -1):
            for h in range(n_freq):
                remote, local, mine, other = descriptor(b, w, h)
                pl.when(other)(remote.start)
                pl.when(mine)(local.start)
        return 0

    lax.fori_loop(0, chunks, transform, 0)

    last_block = chans // owned - 1
    for w in range(n_seg + 1):
        block = z * n_seg + x + w
        row = pl.multiple_of(jnp.minimum(block, last_block) * owned, owned)
        rows = live[pl.ds(row, owned), :]
        lv[w * owned : (w + 1) * owned, :] = jnp.where(block <= last_block, rows, 0.0)
    twice = (
        lax.broadcasted_iota(jnp.int32, (2 * OFFSETS, OFFSETS), 0) // 2
        == lax.broadcasted_iota(jnp.int32, (2 * OFFSETS, OFFSETS), 1)
    ).astype(jnp.float32).astype(jnp.bfloat16)
    ones = jnp.ones((total_segs, half), jnp.bfloat16)

    def count_pairs(i, _):
        both = (lv[pl.ds(i, OFFSETS), :] * lv[pl.ds(i, 1), :]).astype(jnp.bfloat16)
        both = jnp.dot(twice, both, preferred_element_type=jnp.float32).astype(jnp.bfloat16)
        pairs = jnp.dot(both, ones, preferred_element_type=jnp.float32)
        inv[i] = 1.0 / jnp.maximum(pairs, 1.0)
        return 0

    lax.fori_loop(0, owned, count_pairs, 0, unroll=8)

    for part in range(per_granule):
        for sx in range(n_seg):
            arrived(sx, 0, part)

            @pl.when(jnp.logical_and(z > 0, sx != x))
            def _():
                along(sx, part).start()

    for w in range(n_seg, 0, -1):
        for sx in range(n_seg):

            @pl.when(is_hub(sx, w))
            def _():
                for part in range(per_granule):
                    arrived(sx, w, part)
                    for tx in range(n_seg):
                        pl.when(hub_target(sx, w, tx))(across(sx, w, tx, part).start)

    span = n_seg * segs
    row_id = lax.broadcasted_iota(jnp.int32, (2 * KB, KB * span), 0)
    col_id = lax.broadcasted_iota(jnp.int32, (2 * KB, KB * span), 1) // span
    hit = row_id // 2 == col_id
    sum_re = jnp.where(jnp.logical_and(hit, row_id % 2 == 0), 1.0, 0.0).astype(jnp.bfloat16)
    sum_im = jnp.where(jnp.logical_and(hit, row_id % 2 == 1), 1.0, 0.0).astype(jnp.bfloat16)

    sub_parts = KB // CHUNK_CH
    for t in range((n_seg + 1) * owned // KB):
        w, place = divmod(t * KB, owned)
        inside = z + (x + w) // n_seg < n_chan

        @pl.when(inside)
        def _():
            for sx in range(n_seg):
                for part in range(place // CHUNK_CH, place // CHUNK_CH + sub_parts):
                    if w > 0:
                        pl.when(jnp.logical_not(is_hub(sx, w)))(functools.partial(arrived, sx, w, part))

            def merge(m, _):
                rows = pl.ds(pl.multiple_of((place + 2 * m) * segs, 2 * segs), 2 * segs)
                parts = [win[sx, w, rows, :].astype(jnp.float32) for sx in range(n_seg)]
                for e in range(2):
                    whole = jnp.concatenate([p[e * segs : (e + 1) * segs] for p in parts], axis=0)
                    merged[t * KB + 2 * m + e] = whole.astype(jnp.bfloat16)
                return 0

            lax.fori_loop(0, KB // 2, merge, 0, unroll=4)

        @pl.when(jnp.logical_not(inside))
        def _():
            merged[t * KB : (t + 1) * KB] = jnp.zeros((KB,) + merged.shape[1:], jnp.bfloat16)

        groups = [a for a in range(owned // KB) if 0 <= t - 1 - a < OFFSETS // KB]

        def correlate(n, _):
            group = groups[0] + n // KB
            i = groups[0] * KB + n
            kb = t - 1 - group
            own = merged[i]
            other = merged[pl.ds(i + KB * kb, KB)]
            own_re, own_im = own[None, :, :half], own[None, :, half:]
            other_re, other_im = other[:, :, :half], other[:, :, half:]
            re = own_re * other_re + own_im * other_im
            im = own_re * other_im - own_im * other_re
            total = jnp.dot(
                sum_re, re.reshape(KB * span, half), preferred_element_type=jnp.float32
            ) + jnp.dot(sum_im, im.reshape(KB * span, half), preferred_element_type=jnp.float32)
            rows = pl.ds(pl.multiple_of(2 * KB * kb, 2 * KB), 2 * KB)
            out[i, rows, :] = (total * inv[i, rows, :]).astype(jnp.bfloat16)
            return 0

        if groups:
            lax.fori_loop(0, len(groups) * KB, correlate, 0, unroll=8)

    def drain(b, _):
        for w in range(n_seg + 1):
            for h in range(n_freq):
                remote, local, mine, other = descriptor(b, w, h)
                pl.when(other)(remote.wait_send)
        return 0

    lax.fori_loop(0, chunks, drain, 0)
    for part in range(per_granule):
        for sx in range(n_seg):
            pl.when(jnp.logical_and(z > 0, sx != x))(along(sx, part).wait_send)
            for w in range(1, n_seg + 1):
                for tx in range(n_seg):
                    pl.when(hub_target(sx, w, tx))(across(sx, w, tx, part).wait_send)


def shards(samples, live):
    ch_dev, segs, length = samples.shape
    n_chan, n_seg, n_freq = (lax.axis_size(a) for a in ("chan", "seg", "freq"))
    owned = ch_dev // n_seg
    half = BINS // n_freq
    core_ch = ch_dev // n_freq
    chunks = core_ch // CHUNK_CH
    chunk_rows = CHUNK_CH * segs
    quarter = length // QUARTERS
    window = (n_seg + 1) * owned
    result = pl.pallas_call(
        functools.partial(kernel, n_chan, n_seg, n_freq),
        out_shape=jax.ShapeDtypeStruct((owned, 2 * OFFSETS, half), jnp.bfloat16),
        in_specs=[pl.BlockSpec(memory_space=pltpu.HBM)] * 2,
        out_specs=pl.BlockSpec(memory_space=pltpu.VMEM),
        scratch_shapes=[
            pltpu.VMEM(live.shape[::-1], jnp.int32),
            pltpu.VMEM(live.shape, jnp.float32),
            pltpu.VMEM((chunks, QUARTERS * chunk_rows, quarter), jnp.bfloat16),
            pltpu.VMEM((quarter, 2 * BINS), jnp.bfloat16),
            pltpu.VMEM((2, quarter // FINE, BINS), jnp.float32),
            pltpu.VMEM((n_freq, core_ch * segs, 2 * half), jnp.bfloat16),
            pltpu.VMEM((n_seg, n_seg + 1, owned * segs, 2 * half), jnp.bfloat16),
            pltpu.VMEM((window, n_seg * segs, 2 * half), jnp.bfloat16),
            pltpu.VMEM((window, n_seg * segs), jnp.float32),
            pltpu.VMEM((owned, 2 * OFFSETS, half), jnp.float32),
            pltpu.SemaphoreType.DMA,
            pltpu.SemaphoreType.DMA((chunks, QUARTERS)),
            pltpu.SemaphoreType.DMA((chunks, n_seg + 1, n_freq)),
            pltpu.SemaphoreType.DMA((n_seg, n_seg + 1, owned // CHUNK_CH)),
            pltpu.SemaphoreType.DMA((n_seg, owned // CHUNK_CH)),
            pltpu.SemaphoreType.DMA((n_seg, n_seg, n_seg, owned // CHUNK_CH)),
        ],
        compiler_params=pltpu.CompilerParams(
            collective_id=0, has_side_effects=True, vmem_limit_bytes=48 * 1024 * 1024
        ),
    )(samples.reshape(ch_dev * segs, length), live.T)
    return result.reshape(owned, OFFSETS, 2, half)


def solution(mesh):
    return jax.shard_map(
        shards,
        mesh=mesh,
        in_specs=(P(("cable", "chan"), "seg", None), P("cable", None)),
        out_specs=P(("cable", "chan", "seg"), None, None, "freq"),
        check_vma=False,
    )
```

```python
import functools
import math

import jax
import jax.numpy as jnp
from jax import lax
from jax.experimental import pallas as pl
from jax.experimental.pallas import tpu as pltpu
from jax.sharding import PartitionSpec as P

BINS = 256
OFFSETS = 64
EPSILON = 1e-06
QUARTERS = 4
FINE = 64
CHUNK_CH = 8
KB = 16
MESH = pl.DeviceIdType.MESH


def unit_circle(first, step, count, length):
    t = first + step * lax.broadcasted_iota(jnp.int32, (count, BINS), 0)
    k = 1 + lax.broadcasted_iota(jnp.int32, (count, BINS), 1)
    m = lax.rem(t * k, length)
    m = jnp.where(m >= length // 2, m - length, m)
    y = m.astype(jnp.float32) * (math.pi / length)
    y2 = y * y
    sine = jnp.full_like(y, 1.0 / math.factorial(13))
    for order in (11, 9, 7, 5, 3, 1):
        sine = sine * y2 + (-1.0) ** (order // 2) / math.factorial(order)
    sine = sine * y
    cosine = jnp.full_like(y, -1.0 / math.factorial(14))
    for order in (12, 10, 8, 6, 4, 2, 0):
        cosine = cosine * y2 + (-1.0) ** (order // 2) / math.factorial(order)
    return 1.0 - 2.0 * sine * sine, 2.0 * sine * cosine


def kernel(
    n_chan, n_seg, n_freq, samples, live_hbm, out, live_in, live, xs, tab, seeds, snd, win, merged, lv, inv,
    live_sem, x_sem, send_sem, recv_sem, along_sem, across_sem,
):
    length = samples.shape[1]
    quarter = length // QUARTERS
    total_segs, chans = live_in.shape
    ch_dev = chans // n_chan
    segs = samples.shape[0] // ch_dev
    owned = ch_dev // n_seg
    half = BINS // n_freq
    core_ch = ch_dev // n_freq
    gpc = n_seg // n_freq
    chunk_rows = CHUNK_CH * segs
    chunks = core_ch // CHUNK_CH
    per_granule = owned // CHUNK_CH
    z, x, c = lax.axis_index("chan"), lax.axis_index("seg"), lax.axis_index("freq")

    def fetch(b, q):
        row = pl.multiple_of((c * chunks + b) * chunk_rows, chunk_rows)
        return pltpu.make_async_copy(
            samples.at[pl.ds(row, chunk_rows), pl.ds(q * quarter, quarter)],
            xs.at[b, pl.ds(q * chunk_rows, chunk_rows), :],
            x_sem.at[b, q],
        )

    for b in range(chunks):
        for q in range(QUARTERS):
            fetch(b, q).start()
    live_copy = pltpu.make_async_copy(live_hbm, live_in, live_sem)
    live_copy.start()

    barrier = pltpu.get_barrier_semaphore()
    for dz in (-1, 0, 1):
        near = jnp.logical_and(z + dz >= 0, z + dz < n_chan)
        for tx in range(n_seg):
            for tc in range(n_freq):
                other = near if dz else jnp.logical_or(x != tx, c != tc)

                @pl.when(other)
                def _():
                    pl.semaphore_signal(
                        barrier, inc=1, device_id={"chan": z + dz, "seg": tx, "freq": tc},
                        device_id_type=MESH,
                    )

    fine_cos, fine_sin = unit_circle(0, 1, FINE, length)
    coarse_cos, coarse_sin = unit_circle(0, FINE, quarter // FINE, length)
    seeds[0] = coarse_cos
    seeds[1] = coarse_sin

    def table_rows(a, _):
        ca, sa = seeds[0, pl.ds(a, 1), :], seeds[1, pl.ds(a, 1), :]
        rows = pl.ds(pl.multiple_of(a * FINE, FINE), FINE)
        tab[rows, :BINS] = (ca * fine_cos - sa * fine_sin).astype(jnp.bfloat16)
        tab[rows, BINS:] = (-(sa * fine_cos + ca * fine_sin)).astype(jnp.bfloat16)
        return 0

    lax.fori_loop(0, quarter // FINE, table_rows, 0, unroll=4)

    live_copy.wait()
    live[...] = live_in[...].astype(jnp.float32).T
    degree = n_seg * n_freq
    up = (z > 0).astype(jnp.int32)
    down = (z < n_chan - 1).astype(jnp.int32)
    pl.semaphore_wait(barrier, degree - 1 + degree * (up + down))

    def descriptor(b, w, h):
        bb, part = b // per_granule, b % per_granule
        granule = c * gpc + bb
        below = (granule < w).astype(jnp.int32)
        tz, tx = z - below, granule - w + below * n_seg
        rows = pl.ds(pl.multiple_of(b * chunk_rows, chunk_rows), chunk_rows)
        dst_rows = pl.ds(pl.multiple_of(part * chunk_rows, chunk_rows), chunk_rows)
        src = snd.at[h, rows, :]
        dst = win.at[x, w, dst_rows, :]
        remote = pltpu.make_async_remote_copy(
            src_ref=src, dst_ref=dst, send_sem=send_sem.at[b, w, h], recv_sem=recv_sem.at[x, w, part],
            device_id={"chan": tz, "seg": tx, "freq": jnp.int32(h)}, device_id_type=MESH,
        )
        local = pltpu.make_async_copy(src, dst, recv_sem.at[x, w, part])
        mine = jnp.logical_and(jnp.logical_and(tz == z, tx == x), c == h)
        straight = jnp.logical_or(below == 0, jnp.logical_and(tz >= 0, tx == x))
        return remote, local, mine, jnp.logical_and(straight, jnp.logical_not(mine))

    def arrived(sx, w, part):
        dst = win.at[sx, w, pl.ds(part * chunk_rows, chunk_rows), :]
        pltpu.make_async_copy(dst, dst, recv_sem.at[sx, w, part]).wait()

    def relay(sx, w, part, to_w, tz, tx, sem):
        rows = pl.ds(part * chunk_rows, chunk_rows)
        return pltpu.make_async_remote_copy(
            src_ref=win.at[sx, w, rows, :], dst_ref=win.at[sx, to_w, rows, :], send_sem=sem,
            recv_sem=recv_sem.at[sx, to_w, part],
            device_id={"chan": tz, "seg": tx, "freq": c}, device_id_type=MESH,
        )

    def along(sx, part):
        return relay(sx, 0, part, n_seg, z - 1, x, along_sem.at[sx, part])

    def across(sx, w, tx, part):
        return relay(sx, w, part, w + x - tx, z, jnp.int32(tx), across_sem.at[sx, w - 1, tx, part])

    has_above = z < n_chan - 1

    def is_hub(sx, w):
        granule = x + w - n_seg
        own = jnp.logical_and(sx == x, jnp.logical_and(granule >= 0, granule < n_seg - 1))
        own = jnp.logical_and(own, jnp.logical_or(granule < n_seg - 2, x < n_seg - 1))
        first = jnp.logical_and(w == n_seg, jnp.logical_and(sx < x, x < n_seg - 1))
        return jnp.logical_and(has_above, jnp.logical_or(own, first))

    def hub_target(sx, w, tx):
        return jnp.logical_and(is_hub(sx, w), jnp.logical_and(tx > x + w - n_seg, tx != x))

    lane_k = 1 + lax.broadcasted_iota(jnp.int32, (1, BINS), 1)
    phase = lane_k % 4
    alpha = jnp.where(phase == 0, 1.0, jnp.where(phase == 2, -1.0, 0.0))
    beta = jnp.where(phase == 1, 1.0, jnp.where(phase == 3, -1.0, 0.0))
    sigma = jnp.where(lane_k % 2 == 0, 1.0, -1.0)

    def transform(b, _):
        for q in range(QUARTERS):
            fetch(b, q).wait()
        acc = jnp.dot(xs[b], tab[...], preferred_element_type=jnp.float32)
        part = [acc[q * chunk_rows : (q + 1) * chunk_rows] for q in range(QUARTERS)]
        re = [p[:, :BINS] for p in part]
        im = [p[:, BINS:] for p in part]
        odd_re, odd_im = re[1] + sigma * re[3], im[1] + sigma * im[3]
        full_re = re[0] + sigma * re[2] + (alpha * odd_re + beta * odd_im)
        full_im = im[0] + sigma * im[2] + (alpha * odd_im - beta * odd_re)
        energy = jnp.sum(full_re * full_re + full_im * full_im, axis=1, keepdims=True)
        scaling = lax.rsqrt(energy / (2 * BINS) + EPSILON)
        first = pl.multiple_of(z * ch_dev + c * core_ch + b * CHUNK_CH, CHUNK_CH)
        usable = live[pl.ds(first, CHUNK_CH), :]
        usable = jnp.broadcast_to(usable[:, None, :], (CHUNK_CH, segs, total_segs))
        column = lax.broadcasted_iota(jnp.int32, usable.shape, 2)
        segment = x * segs + lax.broadcasted_iota(jnp.int32, usable.shape, 1)
        usable = jnp.where(column == segment, usable, 0.0).reshape(chunk_rows, total_segs)
        usable = jnp.sum(usable, axis=1, keepdims=True)
        white_re = (full_re * scaling * usable).astype(jnp.bfloat16)
        white_im = (full_im * scaling * usable).astype(jnp.bfloat16)
        rows = pl.ds(pl.multiple_of(b * chunk_rows, chunk_rows), chunk_rows)
        for h in range(n_freq):
            snd[h, rows, :half] = white_re[:, h * half : (h + 1) * half]
            snd[h, rows, half:] = white_im[:, h * half : (h + 1) * half]
        for w in range(n_seg, -1, -1):
            for h in range(n_freq):
                remote, local, mine, other = descriptor(b, w, h)
                pl.when(other)(remote.start)
                pl.when(mine)(local.start)
        return 0

    lax.fori_loop(0, chunks, transform, 0)

    last_block = chans // owned - 1
    for w in range(n_seg + 1):
        block = z * n_seg + x + w
        row = pl.multiple_of(jnp.minimum(block, last_block) * owned, owned)
        rows = live[pl.ds(row, owned), :]
        lv[w * owned : (w + 1) * owned, :] = jnp.where(block <= last_block, rows, 0.0)
    twice = (
        lax.broadcasted_iota(jnp.int32, (2 * OFFSETS, OFFSETS), 0) // 2
        == lax.broadcasted_iota(jnp.int32, (2 * OFFSETS, OFFSETS), 1)
    ).astype(jnp.float32).astype(jnp.bfloat16)
    ones = jnp.ones((total_segs, half), jnp.bfloat16)

    def count_pairs(i, _):
        both = (lv[pl.ds(i, OFFSETS), :] * lv[pl.ds(i, 1), :]).astype(jnp.bfloat16)
        both = jnp.dot(twice, both, preferred_element_type=jnp.float32).astype(jnp.bfloat16)
        pairs = jnp.dot(both, ones, preferred_element_type=jnp.float32)
        pairs = jnp.maximum(pairs, 1.0)
        guess = pl.reciprocal(pairs, approx=True)
        inv[i] = guess * (2.0 - pairs * guess)
        return 0

    lax.fori_loop(0, owned, count_pairs, 0, unroll=8)

    for part in range(per_granule):
        for sx in range(n_seg):
            arrived(sx, 0, part)

            @pl.when(jnp.logical_and(z > 0, sx != x))
            def _():
                along(sx, part).start()

    for w in range(n_seg, 0, -1):
        for sx in range(n_seg):

            @pl.when(is_hub(sx, w))
            def _():
                for part in range(per_granule):
                    arrived(sx, w, part)
                    for tx in range(n_seg):
                        pl.when(hub_target(sx, w, tx))(across(sx, w, tx, part).start)

    span = n_seg * segs
    row_id = lax.broadcasted_iota(jnp.int32, (2 * KB, KB * span), 0)
    col_id = lax.broadcasted_iota(jnp.int32, (2 * KB, KB * span), 1) // span
    hit = row_id // 2 == col_id
    sum_re = jnp.where(jnp.logical_and(hit, row_id % 2 == 0), 1.0, 0.0).astype(jnp.bfloat16)
    sum_im = jnp.where(jnp.logical_and(hit, row_id % 2 == 1), 1.0, 0.0).astype(jnp.bfloat16)

    sub_parts = KB // CHUNK_CH
    for t in range((n_seg + 1) * owned // KB):
        w, place = divmod(t * KB, owned)
        inside = z + (x + w) // n_seg < n_chan

        @pl.when(inside)
        def _():
            for sx in range(n_seg):
                for part in range(place // CHUNK_CH, place // CHUNK_CH + sub_parts):
                    if w > 0:
                        pl.when(jnp.logical_not(is_hub(sx, w)))(functools.partial(arrived, sx, w, part))

            def merge(m, _):
                rows = pl.ds(pl.multiple_of((place + 2 * m) * segs, 2 * segs), 2 * segs)
                parts = [win[sx, w, rows, :].astype(jnp.float32) for sx in range(n_seg)]
                for e in range(2):
                    whole = jnp.concatenate([p[e * segs : (e + 1) * segs] for p in parts], axis=0)
                    merged[t * KB + 2 * m + e] = whole.astype(jnp.bfloat16)
                return 0

            lax.fori_loop(0, KB // 2, merge, 0, unroll=4)

        @pl.when(jnp.logical_not(inside))
        def _():
            merged[t * KB : (t + 1) * KB] = jnp.zeros((KB,) + merged.shape[1:], jnp.bfloat16)

        groups = [a for a in range(owned // KB) if 0 <= t - 1 - a < OFFSETS // KB]

        def correlate(n, _):
            group = groups[0] + n // KB
            i = groups[0] * KB + n
            kb = t - 1 - group
            own = merged[i]
            other = merged[pl.ds(i + KB * kb, KB)]
            own_re, own_im = own[None, :, :half], own[None, :, half:]
            other_re, other_im = other[:, :, :half], other[:, :, half:]
            re = own_re * other_re + own_im * other_im
            im = own_re * other_im - own_im * other_re
            total = jnp.dot(
                sum_re, re.reshape(KB * span, half), preferred_element_type=jnp.float32
            ) + jnp.dot(sum_im, im.reshape(KB * span, half), preferred_element_type=jnp.float32)
            rows = pl.ds(pl.multiple_of(2 * KB * kb, 2 * KB), 2 * KB)
            out[i, rows, :] = (total * inv[i, rows, :]).astype(jnp.bfloat16)
            return 0

        if groups:
            lax.fori_loop(0, len(groups) * KB, correlate, 0, unroll=16)

    def drain(b, _):
        for w in range(n_seg + 1):
            for h in range(n_freq):
                remote, local, mine, other = descriptor(b, w, h)
                pl.when(other)(remote.wait_send)
        return 0

    lax.fori_loop(0, chunks, drain, 0)
    for part in range(per_granule):
        for sx in range(n_seg):
            pl.when(jnp.logical_and(z > 0, sx != x))(along(sx, part).wait_send)
            for w in range(1, n_seg + 1):
                for tx in range(n_seg):
                    pl.when(hub_target(sx, w, tx))(across(sx, w, tx, part).wait_send)


def shards(samples, live):
    ch_dev, segs, length = samples.shape
    n_chan, n_seg, n_freq = (lax.axis_size(a) for a in ("chan", "seg", "freq"))
    owned = ch_dev // n_seg
    half = BINS // n_freq
    core_ch = ch_dev // n_freq
    chunks = core_ch // CHUNK_CH
    chunk_rows = CHUNK_CH * segs
    quarter = length // QUARTERS
    window = (n_seg + 1) * owned
    result = pl.pallas_call(
        functools.partial(kernel, n_chan, n_seg, n_freq),
        out_shape=jax.ShapeDtypeStruct((owned, 2 * OFFSETS, half), jnp.bfloat16),
        in_specs=[pl.BlockSpec(memory_space=pltpu.HBM)] * 2,
        out_specs=pl.BlockSpec(memory_space=pltpu.VMEM),
        scratch_shapes=[
            pltpu.VMEM(live.shape[::-1], jnp.int32),
            pltpu.VMEM(live.shape, jnp.float32),
            pltpu.VMEM((chunks, QUARTERS * chunk_rows, quarter), jnp.bfloat16),
            pltpu.VMEM((quarter, 2 * BINS), jnp.bfloat16),
            pltpu.VMEM((2, quarter // FINE, BINS), jnp.float32),
            pltpu.VMEM((n_freq, core_ch * segs, 2 * half), jnp.bfloat16),
            pltpu.VMEM((n_seg, n_seg + 1, owned * segs, 2 * half), jnp.bfloat16),
            pltpu.VMEM((window, n_seg * segs, 2 * half), jnp.bfloat16),
            pltpu.VMEM((window, n_seg * segs), jnp.float32),
            pltpu.VMEM((owned, 2 * OFFSETS, half), jnp.float32),
            pltpu.SemaphoreType.DMA,
            pltpu.SemaphoreType.DMA((chunks, QUARTERS)),
            pltpu.SemaphoreType.DMA((chunks, n_seg + 1, n_freq)),
            pltpu.SemaphoreType.DMA((n_seg, n_seg + 1, owned // CHUNK_CH)),
            pltpu.SemaphoreType.DMA((n_seg, owned // CHUNK_CH)),
            pltpu.SemaphoreType.DMA((n_seg, n_seg, n_seg, owned // CHUNK_CH)),
        ],
        compiler_params=pltpu.CompilerParams(
            collective_id=0, has_side_effects=True, vmem_limit_bytes=48 * 1024 * 1024
        ),
    )(samples.reshape(ch_dev * segs, length), live.T)
    return result.reshape(owned, OFFSETS, 2, half)


def solution(mesh):
    return jax.shard_map(
        shards,
        mesh=mesh,
        in_specs=(P(("cable", "chan"), "seg", None), P("cable", None)),
        out_specs=P(("cable", "chan", "seg"), None, None, "freq"),
        check_vma=False,
    )
```

```python
import functools
import math

import jax
import jax.numpy as jnp
from jax import lax
from jax.experimental import pallas as pl
from jax.experimental.pallas import tpu as pltpu
from jax.sharding import PartitionSpec as P

BINS = 256
OFFSETS = 64
EPSILON = 1e-06
QUARTERS = 4
FINE = 64
CHUNK_CH = 8
KB = 16
MESH = pl.DeviceIdType.MESH


def unit_circle(first, step, count, length):
    t = first + step * lax.broadcasted_iota(jnp.int32, (count, BINS), 0)
    k = 1 + lax.broadcasted_iota(jnp.int32, (count, BINS), 1)
    m = lax.rem(t * k, length)
    m = jnp.where(m >= length // 2, m - length, m)
    y = m.astype(jnp.float32) * (math.pi / length)
    y2 = y * y
    sine = jnp.full_like(y, 1.0 / math.factorial(13))
    for order in (11, 9, 7, 5, 3, 1):
        sine = sine * y2 + (-1.0) ** (order // 2) / math.factorial(order)
    sine = sine * y
    cosine = jnp.full_like(y, -1.0 / math.factorial(14))
    for order in (12, 10, 8, 6, 4, 2, 0):
        cosine = cosine * y2 + (-1.0) ** (order // 2) / math.factorial(order)
    return 1.0 - 2.0 * sine * sine, 2.0 * sine * cosine


def kernel(
    n_chan, n_seg, n_freq, samples, live_hbm, out, live_in, live, xs, tab, seeds, snd, win, merged, lv, inv,
    live_sem, x_sem, send_sem, recv_sem, along_sem, across_sem,
):
    length = samples.shape[1]
    quarter = length // QUARTERS
    total_segs, chans = live_in.shape
    ch_dev = chans // n_chan
    segs = samples.shape[0] // ch_dev
    owned = ch_dev // n_seg
    half = BINS // n_freq
    core_ch = ch_dev // n_freq
    gpc = n_seg // n_freq
    chunk_rows = CHUNK_CH * segs
    chunks = core_ch // CHUNK_CH
    per_granule = owned // CHUNK_CH
    z, x, c = lax.axis_index("chan"), lax.axis_index("seg"), lax.axis_index("freq")

    def fetch(b, q):
        row = pl.multiple_of((c * chunks + b) * chunk_rows, chunk_rows)
        return pltpu.make_async_copy(
            samples.at[pl.ds(row, chunk_rows), pl.ds(q * quarter, quarter)],
            xs.at[b, pl.ds(q * chunk_rows, chunk_rows), :],
            x_sem.at[b, q],
        )

    for b in range(chunks):
        for q in range(QUARTERS):
            fetch(b, q).start()
    live_copy = pltpu.make_async_copy(live_hbm, live_in, live_sem)
    live_copy.start()

    barrier = pltpu.get_barrier_semaphore()
    for dz in (-1, 0, 1):
        near = jnp.logical_and(z + dz >= 0, z + dz < n_chan)
        for tx in range(n_seg):
            for tc in range(n_freq):
                other = near if dz else jnp.logical_or(x != tx, c != tc)

                @pl.when(other)
                def _():
                    pl.semaphore_signal(
                        barrier, inc=1, device_id={"chan": z + dz, "seg": tx, "freq": tc},
                        device_id_type=MESH,
                    )

    fine_cos, fine_sin = unit_circle(0, 1, FINE, length)
    coarse_cos, coarse_sin = unit_circle(0, FINE, quarter // FINE, length)
    seeds[0] = coarse_cos
    seeds[1] = coarse_sin

    def table_rows(a, _):
        ca, sa = seeds[0, pl.ds(a, 1), :], seeds[1, pl.ds(a, 1), :]
        rows = pl.ds(pl.multiple_of(a * FINE, FINE), FINE)
        tab[rows, :BINS] = (ca * fine_cos - sa * fine_sin).astype(jnp.bfloat16)
        tab[rows, BINS:] = (-(sa * fine_cos + ca * fine_sin)).astype(jnp.bfloat16)
        return 0

    lax.fori_loop(0, quarter // FINE, table_rows, 0, unroll=4)

    live_copy.wait()
    live[...] = live_in[...].astype(jnp.float32).T
    degree = n_seg * n_freq
    up = (z > 0).astype(jnp.int32)
    down = (z < n_chan - 1).astype(jnp.int32)
    pl.semaphore_wait(barrier, degree - 1 + degree * (up + down))

    def target(b, w):
        granule = c * gpc + b // per_granule
        below = (granule < w).astype(jnp.int32)
        return z - below, granule - w + below * n_seg, below

    def route(b, w):
        tz, tx, below = target(b, w)
        own = jnp.logical_and(below == 0, tx == x)
        other = jnp.where(below == 0, tx != x, jnp.logical_and(tz >= 0, tx == x))
        return other, own

    def ends(b, w, h):
        part = b % per_granule
        src = snd.at[h, pl.ds(b * chunk_rows, chunk_rows), :]
        dst = win.at[x, w, pl.ds(part * chunk_rows, chunk_rows), :]
        return src, dst, recv_sem.at[x, w, part]

    def descriptor(b, w, h):
        tz, tx, _ = target(b, w)
        src, dst, sem = ends(b, w, h)
        return pltpu.make_async_remote_copy(
            src_ref=src, dst_ref=dst, send_sem=send_sem.at[b, w, h], recv_sem=sem,
            device_id={"chan": tz, "seg": tx, "freq": jnp.int32(h)}, device_id_type=MESH,
        )

    def stay(b, w, h):
        src, dst, sem = ends(b, w, h)
        return pltpu.make_async_copy(src, dst, sem)

    def arrived(sx, w, part):
        dst = win.at[sx, w, pl.ds(part * chunk_rows, chunk_rows), :]
        pltpu.make_async_copy(dst, dst, recv_sem.at[sx, w, part]).wait()

    def relay(sx, w, part, to_w, tz, tx, sem):
        rows = pl.ds(part * chunk_rows, chunk_rows)
        return pltpu.make_async_remote_copy(
            src_ref=win.at[sx, w, rows, :], dst_ref=win.at[sx, to_w, rows, :], send_sem=sem,
            recv_sem=recv_sem.at[sx, to_w, part],
            device_id={"chan": tz, "seg": tx, "freq": c}, device_id_type=MESH,
        )

    def along(sx, part):
        return relay(sx, 0, part, n_seg, z - 1, x, along_sem.at[sx, part])

    def across(sx, w, tx, part):
        return relay(sx, w, part, w + x - tx, z, jnp.int32(tx), across_sem.at[sx, w - 1, tx, part])

    has_above = z < n_chan - 1

    def is_hub(sx, w):
        granule = x + w - n_seg
        own = jnp.logical_and(sx == x, jnp.logical_and(granule >= 0, granule < n_seg - 1))
        own = jnp.logical_and(own, jnp.logical_or(granule < n_seg - 2, x < n_seg - 1))
        first = jnp.logical_and(w == n_seg, jnp.logical_and(sx < x, x < n_seg - 1))
        return jnp.logical_and(has_above, jnp.logical_or(own, first))

    def hub_target(sx, w, tx):
        return jnp.logical_and(is_hub(sx, w), jnp.logical_and(tx > x + w - n_seg, tx != x))

    lane_k = 1 + lax.broadcasted_iota(jnp.int32, (1, BINS), 1)
    phase = lane_k % 4
    alpha = jnp.where(phase == 0, 1.0, jnp.where(phase == 2, -1.0, 0.0))
    beta = jnp.where(phase == 1, 1.0, jnp.where(phase == 3, -1.0, 0.0))
    sigma = jnp.where(lane_k % 2 == 0, 1.0, -1.0)

    def product(b):
        for q in range(QUARTERS):
            fetch(b, q).wait()
        return jnp.dot(xs[b], tab[...], preferred_element_type=jnp.float32)

    def whiten(b, acc):
        part = [acc[q * chunk_rows : (q + 1) * chunk_rows] for q in range(QUARTERS)]
        re = [p[:, :BINS] for p in part]
        im = [p[:, BINS:] for p in part]
        odd_re, odd_im = re[1] + sigma * re[3], im[1] + sigma * im[3]
        full_re = re[0] + sigma * re[2] + (alpha * odd_re + beta * odd_im)
        full_im = im[0] + sigma * im[2] + (alpha * odd_im - beta * odd_re)
        energy = jnp.sum(full_re * full_re + full_im * full_im, axis=1, keepdims=True)
        scaling = lax.rsqrt(energy / (2 * BINS) + EPSILON)
        first = pl.multiple_of(z * ch_dev + c * core_ch + b * CHUNK_CH, CHUNK_CH)
        usable = live[pl.ds(first, CHUNK_CH), :]
        usable = jnp.broadcast_to(usable[:, None, :], (CHUNK_CH, segs, total_segs))
        column = lax.broadcasted_iota(jnp.int32, usable.shape, 2)
        segment = x * segs + lax.broadcasted_iota(jnp.int32, usable.shape, 1)
        usable = jnp.where(column == segment, usable, 0.0).reshape(chunk_rows, total_segs)
        usable = jnp.sum(usable, axis=1, keepdims=True)
        white_re = (full_re * scaling * usable).astype(jnp.bfloat16)
        white_im = (full_im * scaling * usable).astype(jnp.bfloat16)
        rows = slice(b * chunk_rows, (b + 1) * chunk_rows)
        for h in range(n_freq):
            snd[h, rows, :half] = white_re[:, h * half : (h + 1) * half]
            snd[h, rows, half:] = white_im[:, h * half : (h + 1) * half]

    def send(b):
        for w in range(n_seg, -1, -1):
            straight, own = route(b, w)

            @pl.when(straight)
            def _():
                for h in range(n_freq):
                    descriptor(b, w, h).start()

            @pl.when(own)
            def _():
                for h in range(n_freq):
                    pl.when(c != h)(descriptor(b, w, h).start)
                    pl.when(c == h)(stay(b, w, h).start)

    acc = product(0)
    for b in range(chunks):
        following = product(b + 1) if b + 1 < chunks else None
        whiten(b, acc)
        send(b)
        acc = following

    last_block = chans // owned - 1
    for w in range(n_seg + 1):
        block = z * n_seg + x + w
        row = pl.multiple_of(jnp.minimum(block, last_block) * owned, owned)
        rows = live[pl.ds(row, owned), :]
        lv[w * owned : (w + 1) * owned, :] = jnp.where(block <= last_block, rows, 0.0)
    twice = (
        lax.broadcasted_iota(jnp.int32, (2 * OFFSETS, OFFSETS), 0) // 2
        == lax.broadcasted_iota(jnp.int32, (2 * OFFSETS, OFFSETS), 1)
    ).astype(jnp.float32).astype(jnp.bfloat16)
    ones = jnp.ones((total_segs, half), jnp.bfloat16)

    def count_pairs(i, _):
        both = (lv[pl.ds(i, OFFSETS), :] * lv[pl.ds(i, 1), :]).astype(jnp.bfloat16)
        both = jnp.dot(twice, both, preferred_element_type=jnp.float32).astype(jnp.bfloat16)
        pairs = jnp.dot(both, ones, preferred_element_type=jnp.float32)
        pairs = jnp.maximum(pairs, 1.0)
        guess = pl.reciprocal(pairs, approx=True)
        inv[i] = guess * (2.0 - pairs * guess)
        return 0

    lax.fori_loop(0, owned, count_pairs, 0, unroll=8)

    for part in range(per_granule):
        for sx in range(n_seg):
            arrived(sx, 0, part)

            @pl.when(jnp.logical_and(z > 0, sx != x))
            def _():
                along(sx, part).start()

    for w in range(n_seg, 0, -1):
        for sx in range(n_seg):

            @pl.when(is_hub(sx, w))
            def _():
                for part in range(per_granule):
                    arrived(sx, w, part)
                    for tx in range(n_seg):
                        pl.when(hub_target(sx, w, tx))(across(sx, w, tx, part).start)

    span = n_seg * segs
    row_id = lax.broadcasted_iota(jnp.int32, (2 * KB, KB * span), 0)
    col_id = lax.broadcasted_iota(jnp.int32, (2 * KB, KB * span), 1) // span
    hit = row_id // 2 == col_id
    sum_re = jnp.where(jnp.logical_and(hit, row_id % 2 == 0), 1.0, 0.0).astype(jnp.bfloat16)
    sum_im = jnp.where(jnp.logical_and(hit, row_id % 2 == 1), 1.0, 0.0).astype(jnp.bfloat16)

    sub_parts = KB // CHUNK_CH
    for t in range((n_seg + 1) * owned // KB):
        w, place = divmod(t * KB, owned)
        inside = z + (x + w) // n_seg < n_chan

        @pl.when(inside)
        def _():
            for sx in range(n_seg):
                for part in range(place // CHUNK_CH, place // CHUNK_CH + sub_parts):
                    if w > 0:
                        pl.when(jnp.logical_not(is_hub(sx, w)))(functools.partial(arrived, sx, w, part))

            def merge(m, _):
                rows = pl.ds(pl.multiple_of((place + 2 * m) * segs, 2 * segs), 2 * segs)
                parts = [win[sx, w, rows, :].astype(jnp.float32) for sx in range(n_seg)]
                for e in range(2):
                    whole = jnp.concatenate([p[e * segs : (e + 1) * segs] for p in parts], axis=0)
                    merged[t * KB + 2 * m + e] = whole.astype(jnp.bfloat16)
                return 0

            lax.fori_loop(0, KB // 2, merge, 0, unroll=4)

        @pl.when(jnp.logical_not(inside))
        def _():
            merged[t * KB : (t + 1) * KB] = jnp.zeros((KB,) + merged.shape[1:], jnp.bfloat16)

        groups = [a for a in range(owned // KB) if 0 <= t - 1 - a < OFFSETS // KB]

        def correlate(n, _):
            group = groups[0] + n // KB
            i = groups[0] * KB + n
            kb = t - 1 - group
            own = merged[i]
            other = merged[pl.ds(i + KB * kb, KB)]
            own_re, own_im = own[None, :, :half], own[None, :, half:]
            other_re, other_im = other[:, :, :half], other[:, :, half:]
            re = own_re * other_re + own_im * other_im
            im = own_re * other_im - own_im * other_re
            total = jnp.dot(
                sum_re, re.reshape(KB * span, half), preferred_element_type=jnp.float32
            ) + jnp.dot(sum_im, im.reshape(KB * span, half), preferred_element_type=jnp.float32)
            rows = pl.ds(pl.multiple_of(2 * KB * kb, 2 * KB), 2 * KB)
            out[i, rows, :] = (total * inv[i, rows, :]).astype(jnp.bfloat16)
            return 0

        if groups:
            lax.fori_loop(0, len(groups) * KB, correlate, 0, unroll=16)

    for b in range(chunks):
        for w in range(n_seg + 1):
            straight, own = route(b, w)
            for h in range(n_freq):
                sent = jnp.logical_or(straight, jnp.logical_and(own, c != h))
                pl.when(sent)(descriptor(b, w, h).wait_send)
    for part in range(per_granule):
        for sx in range(n_seg):
            pl.when(jnp.logical_and(z > 0, sx != x))(along(sx, part).wait_send)
            for w in range(1, n_seg + 1):
                for tx in range(n_seg):
                    pl.when(hub_target(sx, w, tx))(across(sx, w, tx, part).wait_send)


def shards(samples, live):
    ch_dev, segs, length = samples.shape
    n_chan, n_seg, n_freq = (lax.axis_size(a) for a in ("chan", "seg", "freq"))
    owned = ch_dev // n_seg
    half = BINS // n_freq
    core_ch = ch_dev // n_freq
    chunks = core_ch // CHUNK_CH
    chunk_rows = CHUNK_CH * segs
    quarter = length // QUARTERS
    window = (n_seg + 1) * owned
    result = pl.pallas_call(
        functools.partial(kernel, n_chan, n_seg, n_freq),
        out_shape=jax.ShapeDtypeStruct((owned, 2 * OFFSETS, half), jnp.bfloat16),
        in_specs=[pl.BlockSpec(memory_space=pltpu.HBM)] * 2,
        out_specs=pl.BlockSpec(memory_space=pltpu.VMEM),
        scratch_shapes=[
            pltpu.VMEM(live.shape[::-1], jnp.int32),
            pltpu.VMEM(live.shape, jnp.float32),
            pltpu.VMEM((chunks, QUARTERS * chunk_rows, quarter), jnp.bfloat16),
            pltpu.VMEM((quarter, 2 * BINS), jnp.bfloat16),
            pltpu.VMEM((2, quarter // FINE, BINS), jnp.float32),
            pltpu.VMEM((n_freq, core_ch * segs, 2 * half), jnp.bfloat16),
            pltpu.VMEM((n_seg, n_seg + 1, owned * segs, 2 * half), jnp.bfloat16),
            pltpu.VMEM((window, n_seg * segs, 2 * half), jnp.bfloat16),
            pltpu.VMEM((window, n_seg * segs), jnp.float32),
            pltpu.VMEM((owned, 2 * OFFSETS, half), jnp.float32),
            pltpu.SemaphoreType.DMA,
            pltpu.SemaphoreType.DMA((chunks, QUARTERS)),
            pltpu.SemaphoreType.DMA((chunks, n_seg + 1, n_freq)),
            pltpu.SemaphoreType.DMA((n_seg, n_seg + 1, owned // CHUNK_CH)),
            pltpu.SemaphoreType.DMA((n_seg, owned // CHUNK_CH)),
            pltpu.SemaphoreType.DMA((n_seg, n_seg, n_seg, owned // CHUNK_CH)),
        ],
        compiler_params=pltpu.CompilerParams(
            collective_id=0, has_side_effects=True, vmem_limit_bytes=48 * 1024 * 1024
        ),
    )(samples.reshape(ch_dev * segs, length), live.T)
    return result.reshape(owned, OFFSETS, 2, half)


def solution(mesh):
    return jax.shard_map(
        shards,
        mesh=mesh,
        in_specs=(P(("cable", "chan"), "seg", None), P("cable", None)),
        out_specs=P(("cable", "chan", "seg"), None, None, "freq"),
        check_vma=False,
    )
```

```python
import functools
import math

import jax
import jax.numpy as jnp
from jax import lax
from jax.experimental import pallas as pl
from jax.experimental.pallas import tpu as pltpu
from jax.sharding import PartitionSpec as P

BINS = 256
OFFSETS = 64
EPSILON = 1e-06
QUARTERS = 4
FINE = 64
CHUNK_CH = 8
KB = 16
MESH = pl.DeviceIdType.MESH


def unit_circle(first, step, count, length):
    t = first + step * lax.broadcasted_iota(jnp.int32, (count, BINS), 0)
    k = 1 + lax.broadcasted_iota(jnp.int32, (count, BINS), 1)
    m = lax.rem(t * k, length)
    m = jnp.where(m >= length // 2, m - length, m)
    y = m.astype(jnp.float32) * (math.pi / length)
    y2 = y * y
    sine = jnp.full_like(y, 1.0 / math.factorial(13))
    for order in (11, 9, 7, 5, 3, 1):
        sine = sine * y2 + (-1.0) ** (order // 2) / math.factorial(order)
    sine = sine * y
    cosine = jnp.full_like(y, -1.0 / math.factorial(14))
    for order in (12, 10, 8, 6, 4, 2, 0):
        cosine = cosine * y2 + (-1.0) ** (order // 2) / math.factorial(order)
    return 1.0 - 2.0 * sine * sine, 2.0 * sine * cosine


def kernel(
    n_chan, n_seg, n_freq, samples, live_hbm, out, live_in, live, xs, tab, seeds, snd, win, merged, lv, inv,
    live_sem, x_sem, send_sem, recv_sem, along_sem, across_sem,
    side, side_recv, side_send,
):
    length = samples.shape[1]
    quarter = length // QUARTERS
    total_segs, chans = live_in.shape
    ch_dev = chans // n_chan
    segs = samples.shape[0] // ch_dev
    owned = ch_dev // n_seg
    half = BINS // n_freq
    core_ch = ch_dev // n_freq
    gpc = n_seg // n_freq
    chunk_rows = CHUNK_CH * segs
    chunks = core_ch // CHUNK_CH
    per_granule = owned // CHUNK_CH
    z, x, c = lax.axis_index("chan"), lax.axis_index("seg"), lax.axis_index("freq")

    def fetch(b, q):
        row = pl.multiple_of((c * chunks + b) * chunk_rows, chunk_rows)
        return pltpu.make_async_copy(
            samples.at[pl.ds(row, chunk_rows), pl.ds(q * quarter, quarter)],
            xs.at[b, pl.ds(q * chunk_rows, chunk_rows), :],
            x_sem.at[b, q],
        )

    for b in range(chunks):
        for q in range(QUARTERS):
            fetch(b, q).start()
    live_copy = pltpu.make_async_copy(live_hbm, live_in, live_sem)
    live_copy.start()

    barrier = pltpu.get_barrier_semaphore()
    for dz in (-1, 0, 1):
        near = jnp.logical_and(z + dz >= 0, z + dz < n_chan)
        for tx in range(n_seg):
            for tc in range(n_freq):
                other = near if dz else jnp.logical_or(x != tx, c != tc)

                @pl.when(other)
                def _():
                    pl.semaphore_signal(
                        barrier, inc=1, device_id={"chan": z + dz, "seg": tx, "freq": tc},
                        device_id_type=MESH,
                    )

    fine_cos, fine_sin = unit_circle(0, 1, FINE, length)
    coarse_cos, coarse_sin = unit_circle(0, FINE, quarter // FINE, length)
    seeds[0] = coarse_cos
    seeds[1] = coarse_sin

    def table_rows(a, _):
        ca, sa = seeds[0, pl.ds(a, 1), :], seeds[1, pl.ds(a, 1), :]
        rows = pl.ds(pl.multiple_of(a * FINE, FINE), FINE)
        tab[rows, :BINS] = (ca * fine_cos - sa * fine_sin).astype(jnp.bfloat16)
        tab[rows, BINS:] = (-(sa * fine_cos + ca * fine_sin)).astype(jnp.bfloat16)
        return 0

    lax.fori_loop(0, quarter // FINE, table_rows, 0, unroll=4)

    live_copy.wait()
    live[...] = live_in[...].astype(jnp.float32).T
    degree = n_seg * n_freq
    up = (z > 0).astype(jnp.int32)
    down = (z < n_chan - 1).astype(jnp.int32)
    pl.semaphore_wait(barrier, degree - 1 + degree * (up + down))

    def descriptor(b, w, h):
        bb, part = b // per_granule, b % per_granule
        granule = c * gpc + bb
        below = (granule < w).astype(jnp.int32)
        tz, tx = z - below, granule - w + below * n_seg
        rows = pl.ds(pl.multiple_of(b * chunk_rows, chunk_rows), chunk_rows)
        dst_rows = pl.ds(pl.multiple_of(part * chunk_rows, chunk_rows), chunk_rows)
        src = snd.at[h, rows, :]
        dst = win.at[x, w, dst_rows, :]
        remote = pltpu.make_async_remote_copy(
            src_ref=src, dst_ref=dst, send_sem=send_sem.at[b, w, h], recv_sem=recv_sem.at[x, w, part],
            device_id={"chan": tz, "seg": tx, "freq": jnp.int32(h)}, device_id_type=MESH,
        )
        local = pltpu.make_async_copy(src, dst, recv_sem.at[x, w, part])
        mine = jnp.logical_and(jnp.logical_and(tz == z, tx == x), c == h)
        straight = jnp.logical_or(below == 0, jnp.logical_and(tz >= 0, tx == x))
        return remote, local, mine, jnp.logical_and(straight, jnp.logical_not(mine))

    half_way = per_granule // 2 if n_seg == 2 and n_freq == 2 else per_granule

    def detour(b, h):
        part = b % per_granule
        rows = pl.ds(pl.multiple_of(b * chunk_rows, chunk_rows), chunk_rows)
        slot = jnp.maximum(part - half_way, 0)
        copy = pltpu.make_async_remote_copy(
            src_ref=snd.at[h, rows, :], dst_ref=side.at[slot], send_sem=send_sem.at[b, n_seg, h],
            recv_sem=side_recv.at[slot],
            device_id={"chan": z - 1, "seg": x, "freq": jnp.int32(h)}, device_id_type=MESH,
        )
        last = c * gpc + b // per_granule == n_seg - 1
        used = jnp.logical_and(jnp.logical_and(z > 0, x == 0), jnp.logical_and(last, part >= half_way))
        return copy, used

    def onward(slot):
        rows = pl.ds((half_way + slot) * chunk_rows, chunk_rows)
        copy = pltpu.make_async_remote_copy(
            src_ref=side.at[slot], dst_ref=win.at[0, n_seg, rows, :], send_sem=side_send.at[slot],
            recv_sem=recv_sem.at[0, n_seg, half_way + slot],
            device_id={"chan": z, "seg": jnp.int32(n_seg - 1), "freq": c}, device_id_type=MESH,
        )
        return copy, jnp.logical_and(z < n_chan - 1, x == 0)

    def along_used(sx, part):
        used = jnp.logical_and(z > 0, sx != x)
        if part >= half_way and sx == 0:
            used = jnp.logical_and(used, x != n_seg - 1)
        return used

    def arrived(sx, w, part):
        dst = win.at[sx, w, pl.ds(part * chunk_rows, chunk_rows), :]
        pltpu.make_async_copy(dst, dst, recv_sem.at[sx, w, part]).wait()

    def relay(sx, w, part, to_w, tz, tx, sem):
        rows = pl.ds(part * chunk_rows, chunk_rows)
        return pltpu.make_async_remote_copy(
            src_ref=win.at[sx, w, rows, :], dst_ref=win.at[sx, to_w, rows, :], send_sem=sem,
            recv_sem=recv_sem.at[sx, to_w, part],
            device_id={"chan": tz, "seg": tx, "freq": c}, device_id_type=MESH,
        )

    def along(sx, part):
        return relay(sx, 0, part, n_seg, z - 1, x, along_sem.at[sx, part])

    def across(sx, w, tx, part):
        return relay(sx, w, part, w + x - tx, z, jnp.int32(tx), across_sem.at[sx, w - 1, tx, part])

    has_above = z < n_chan - 1

    def is_hub(sx, w):
        granule = x + w - n_seg
        own = jnp.logical_and(sx == x, jnp.logical_and(granule >= 0, granule < n_seg - 1))
        own = jnp.logical_and(own, jnp.logical_or(granule < n_seg - 2, x < n_seg - 1))
        first = jnp.logical_and(w == n_seg, jnp.logical_and(sx < x, x < n_seg - 1))
        return jnp.logical_and(has_above, jnp.logical_or(own, first))

    def hub_target(sx, w, tx):
        return jnp.logical_and(is_hub(sx, w), jnp.logical_and(tx > x + w - n_seg, tx != x))

    lane_k = 1 + lax.broadcasted_iota(jnp.int32, (1, BINS), 1)
    phase = lane_k % 4
    alpha = jnp.where(phase == 0, 1.0, jnp.where(phase == 2, -1.0, 0.0))
    beta = jnp.where(phase == 1, 1.0, jnp.where(phase == 3, -1.0, 0.0))
    sigma = jnp.where(lane_k % 2 == 0, 1.0, -1.0)

    def transform(b, _):
        for q in range(QUARTERS):
            fetch(b, q).wait()
        acc = jnp.dot(xs[b], tab[...], preferred_element_type=jnp.float32)
        part = [acc[q * chunk_rows : (q + 1) * chunk_rows] for q in range(QUARTERS)]
        re = [p[:, :BINS] for p in part]
        im = [p[:, BINS:] for p in part]
        odd_re, odd_im = re[1] + sigma * re[3], im[1] + sigma * im[3]
        full_re = re[0] + sigma * re[2] + (alpha * odd_re + beta * odd_im)
        full_im = im[0] + sigma * im[2] + (alpha * odd_im - beta * odd_re)
        energy = jnp.sum(full_re * full_re + full_im * full_im, axis=1, keepdims=True)
        scaling = lax.rsqrt(energy / (2 * BINS) + EPSILON)
        first = pl.multiple_of(z * ch_dev + c * core_ch + b * CHUNK_CH, CHUNK_CH)
        usable = live[pl.ds(first, CHUNK_CH), :]
        usable = jnp.broadcast_to(usable[:, None, :], (CHUNK_CH, segs, total_segs))
        column = lax.broadcasted_iota(jnp.int32, usable.shape, 2)
        segment = x * segs + lax.broadcasted_iota(jnp.int32, usable.shape, 1)
        usable = jnp.where(column == segment, usable, 0.0).reshape(chunk_rows, total_segs)
        usable = jnp.sum(usable, axis=1, keepdims=True)
        white_re = (full_re * scaling * usable).astype(jnp.bfloat16)
        white_im = (full_im * scaling * usable).astype(jnp.bfloat16)
        rows = pl.ds(pl.multiple_of(b * chunk_rows, chunk_rows), chunk_rows)
        for h in range(n_freq):
            snd[h, rows, :half] = white_re[:, h * half : (h + 1) * half]
            snd[h, rows, half:] = white_im[:, h * half : (h + 1) * half]
        for w in range(n_seg, -1, -1):
            for h in range(n_freq):
                remote, local, mine, other = descriptor(b, w, h)
                pl.when(other)(remote.start)
                pl.when(mine)(local.start)
        if half_way < per_granule:
            for h in range(n_freq):
                copy, used = detour(b, h)
                pl.when(used)(copy.start)
        return 0

    lax.fori_loop(0, chunks, transform, 0)

    last_block = chans // owned - 1
    for w in range(n_seg + 1):
        block = z * n_seg + x + w
        row = pl.multiple_of(jnp.minimum(block, last_block) * owned, owned)
        rows = live[pl.ds(row, owned), :]
        lv[w * owned : (w + 1) * owned, :] = jnp.where(block <= last_block, rows, 0.0)
    twice = (
        lax.broadcasted_iota(jnp.int32, (2 * OFFSETS, OFFSETS), 0) // 2
        == lax.broadcasted_iota(jnp.int32, (2 * OFFSETS, OFFSETS), 1)
    ).astype(jnp.float32).astype(jnp.bfloat16)
    ones = jnp.ones((total_segs, half), jnp.bfloat16)

    def count_pairs(i, _):
        both = (lv[pl.ds(i, OFFSETS), :] * lv[pl.ds(i, 1), :]).astype(jnp.bfloat16)
        both = jnp.dot(twice, both, preferred_element_type=jnp.float32).astype(jnp.bfloat16)
        pairs = jnp.dot(both, ones, preferred_element_type=jnp.float32)
        pairs = jnp.maximum(pairs, 1.0)
        guess = pl.reciprocal(pairs, approx=True)
        inv[i] = guess * (2.0 - pairs * guess)
        return 0

    for part in range(per_granule):
        lax.fori_loop(part * CHUNK_CH, (part + 1) * CHUNK_CH, count_pairs, 0, unroll=CHUNK_CH)
        for w in range(n_seg, 0, -1):
            for sx in range(n_seg):

                @pl.when(is_hub(sx, w))
                def _():
                    arrived(sx, w, part)
                    for tx in range(n_seg):
                        pl.when(hub_target(sx, w, tx))(across(sx, w, tx, part).start)

        for sx in range(n_seg):
            arrived(sx, 0, part)
            pl.when(along_used(sx, part))(along(sx, part).start)

        if part >= half_way:
            copy, used = onward(part - half_way)

            @pl.when(used)
            def _():
                place = side.at[part - half_way]
                pltpu.make_async_copy(place, place, side_recv.at[part - half_way]).wait()
                copy.start()

    span = n_seg * segs
    row_id = lax.broadcasted_iota(jnp.int32, (2 * KB, KB * span), 0)
    col_id = lax.broadcasted_iota(jnp.int32, (2 * KB, KB * span), 1) // span
    hit = row_id // 2 == col_id
    sum_re = jnp.where(jnp.logical_and(hit, row_id % 2 == 0), 1.0, 0.0).astype(jnp.bfloat16)
    sum_im = jnp.where(jnp.logical_and(hit, row_id % 2 == 1), 1.0, 0.0).astype(jnp.bfloat16)

    sub_parts = KB // CHUNK_CH
    for t in range((n_seg + 1) * owned // KB):
        w, place = divmod(t * KB, owned)
        inside = z + (x + w) // n_seg < n_chan

        @pl.when(inside)
        def _():
            for sx in range(n_seg):
                for part in range(place // CHUNK_CH, place // CHUNK_CH + sub_parts):
                    if w > 0:
                        pl.when(jnp.logical_not(is_hub(sx, w)))(functools.partial(arrived, sx, w, part))

            def merge(m, _):
                rows = pl.ds(pl.multiple_of((place + 2 * m) * segs, 2 * segs), 2 * segs)
                parts = [win[sx, w, rows, :].astype(jnp.float32) for sx in range(n_seg)]
                for e in range(2):
                    whole = jnp.concatenate([p[e * segs : (e + 1) * segs] for p in parts], axis=0)
                    merged[t * KB + 2 * m + e] = whole.astype(jnp.bfloat16)
                return 0

            lax.fori_loop(0, KB // 2, merge, 0, unroll=4)

        @pl.when(jnp.logical_not(inside))
        def _():
            merged[t * KB : (t + 1) * KB] = jnp.zeros((KB,) + merged.shape[1:], jnp.bfloat16)

        groups = [a for a in range(owned // KB) if 0 <= t - 1 - a < OFFSETS // KB]

        def correlate(n, _):
            group = groups[0] + n // KB
            i = groups[0] * KB + n
            kb = t - 1 - group
            own = merged[i]
            other = merged[pl.ds(i + KB * kb, KB)]
            own_re, own_im = own[None, :, :half], own[None, :, half:]
            other_re, other_im = other[:, :, :half], other[:, :, half:]
            re = own_re * other_re + own_im * other_im
            im = own_re * other_im - own_im * other_re
            total = jnp.dot(
                sum_re, re.reshape(KB * span, half), preferred_element_type=jnp.float32
            ) + jnp.dot(sum_im, im.reshape(KB * span, half), preferred_element_type=jnp.float32)
            rows = pl.ds(pl.multiple_of(2 * KB * kb, 2 * KB), 2 * KB)
            out[i, rows, :] = (total * inv[i, rows, :]).astype(jnp.bfloat16)
            return 0

        if groups:
            lax.fori_loop(0, len(groups) * KB, correlate, 0, unroll=16)

    def drain(b, _):
        for w in range(n_seg + 1):
            for h in range(n_freq):
                remote, local, mine, other = descriptor(b, w, h)
                pl.when(other)(remote.wait_send)
        if half_way < per_granule:
            for h in range(n_freq):
                copy, used = detour(b, h)
                pl.when(used)(copy.wait_send)
        return 0

    lax.fori_loop(0, chunks, drain, 0)
    for slot in range(per_granule - half_way):
        copy, used = onward(slot)
        pl.when(used)(copy.wait_send)
    for part in range(per_granule):
        for sx in range(n_seg):
            pl.when(along_used(sx, part))(along(sx, part).wait_send)
            for w in range(1, n_seg + 1):
                for tx in range(n_seg):
                    pl.when(hub_target(sx, w, tx))(across(sx, w, tx, part).wait_send)


def shards(samples, live):
    ch_dev, segs, length = samples.shape
    n_chan, n_seg, n_freq = (lax.axis_size(a) for a in ("chan", "seg", "freq"))
    owned = ch_dev // n_seg
    half = BINS // n_freq
    core_ch = ch_dev // n_freq
    chunks = core_ch // CHUNK_CH
    chunk_rows = CHUNK_CH * segs
    quarter = length // QUARTERS
    window = (n_seg + 1) * owned
    result = pl.pallas_call(
        functools.partial(kernel, n_chan, n_seg, n_freq),
        out_shape=jax.ShapeDtypeStruct((owned, 2 * OFFSETS, half), jnp.bfloat16),
        in_specs=[pl.BlockSpec(memory_space=pltpu.HBM)] * 2,
        out_specs=pl.BlockSpec(memory_space=pltpu.VMEM),
        scratch_shapes=[
            pltpu.VMEM(live.shape[::-1], jnp.int32),
            pltpu.VMEM(live.shape, jnp.float32),
            pltpu.VMEM((chunks, QUARTERS * chunk_rows, quarter), jnp.bfloat16),
            pltpu.VMEM((quarter, 2 * BINS), jnp.bfloat16),
            pltpu.VMEM((2, quarter // FINE, BINS), jnp.float32),
            pltpu.VMEM((n_freq, core_ch * segs, 2 * half), jnp.bfloat16),
            pltpu.VMEM((n_seg, n_seg + 1, owned * segs, 2 * half), jnp.bfloat16),
            pltpu.VMEM((window, n_seg * segs, 2 * half), jnp.bfloat16),
            pltpu.VMEM((window, n_seg * segs), jnp.float32),
            pltpu.VMEM((owned, 2 * OFFSETS, half), jnp.float32),
            pltpu.SemaphoreType.DMA,
            pltpu.SemaphoreType.DMA((chunks, QUARTERS)),
            pltpu.SemaphoreType.DMA((chunks, n_seg + 1, n_freq)),
            pltpu.SemaphoreType.DMA((n_seg, n_seg + 1, owned // CHUNK_CH)),
            pltpu.SemaphoreType.DMA((n_seg, owned // CHUNK_CH)),
            pltpu.SemaphoreType.DMA((n_seg, n_seg, n_seg, owned // CHUNK_CH)),
            pltpu.VMEM((owned // CHUNK_CH, chunk_rows, 2 * half), jnp.bfloat16),
            pltpu.SemaphoreType.DMA((owned // CHUNK_CH,)),
            pltpu.SemaphoreType.DMA((owned // CHUNK_CH,)),
        ],
        compiler_params=pltpu.CompilerParams(
            collective_id=0, has_side_effects=True, vmem_limit_bytes=48 * 1024 * 1024
        ),
    )(samples.reshape(ch_dev * segs, length), live.T)
    return result.reshape(owned, OFFSETS, 2, half)


def solution(mesh):
    return jax.shard_map(
        shards,
        mesh=mesh,
        in_specs=(P(("cable", "chan"), "seg", None), P("cable", None)),
        out_specs=P(("cable", "chan", "seg"), None, None, "freq"),
        check_vma=False,
    )
```

```python
import functools
import math

import jax
import jax.numpy as jnp
from jax import lax
from jax.experimental import pallas as pl
from jax.experimental.pallas import tpu as pltpu
from jax.sharding import PartitionSpec as P

BINS = 256
OFFSETS = 64
EPSILON = 1e-06
QUARTERS = 4
FINE = 64
CHUNK_CH = 8
KB = 16
MESH = pl.DeviceIdType.MESH


def unit_circle(first, step, count, length):
    t = first + step * lax.broadcasted_iota(jnp.int32, (count, BINS), 0)
    k = 1 + lax.broadcasted_iota(jnp.int32, (count, BINS), 1)
    m = lax.rem(t * k, length)
    m = jnp.where(m >= length // 2, m - length, m)
    y = m.astype(jnp.float32) * (math.pi / length)
    y2 = y * y
    sine = jnp.full_like(y, 1.0 / math.factorial(13))
    for order in (11, 9, 7, 5, 3, 1):
        sine = sine * y2 + (-1.0) ** (order // 2) / math.factorial(order)
    sine = sine * y
    cosine = jnp.full_like(y, -1.0 / math.factorial(14))
    for order in (12, 10, 8, 6, 4, 2, 0):
        cosine = cosine * y2 + (-1.0) ** (order // 2) / math.factorial(order)
    return 1.0 - 2.0 * sine * sine, 2.0 * sine * cosine


def kernel(
    n_chan, n_seg, n_freq, samples, live_hbm, out, live_in, live, xs, tab, seeds, snd, win, merged, lv, inv,
    live_sem, x_sem, send_sem, recv_sem, along_sem, across_sem,
    side, side_recv, side_send,
):
    length = samples.shape[1]
    quarter = length // QUARTERS
    total_segs, chans = live_in.shape
    ch_dev = chans // n_chan
    segs = samples.shape[0] // ch_dev
    owned = ch_dev // n_seg
    half = BINS // n_freq
    core_ch = ch_dev // n_freq
    gpc = n_seg // n_freq
    chunk_rows = CHUNK_CH * segs
    chunks = core_ch // CHUNK_CH
    per_granule = owned // CHUNK_CH
    z, x, c = lax.axis_index("chan"), lax.axis_index("seg"), lax.axis_index("freq")

    def fetch(b, q):
        row = pl.multiple_of((c * chunks + b) * chunk_rows, chunk_rows)
        return pltpu.make_async_copy(
            samples.at[pl.ds(row, chunk_rows), pl.ds(q * quarter, quarter)],
            xs.at[b, pl.ds(q * chunk_rows, chunk_rows), :],
            x_sem.at[b, q],
        )

    for b in range(chunks):
        for q in range(QUARTERS):
            fetch(b, q).start()
    live_copy = pltpu.make_async_copy(live_hbm, live_in, live_sem)
    live_copy.start()

    barrier = pltpu.get_barrier_semaphore()
    for dz in (-1, 0, 1):
        near = jnp.logical_and(z + dz >= 0, z + dz < n_chan)
        for tx in range(n_seg):
            for tc in range(n_freq):
                other = near if dz else jnp.logical_or(x != tx, c != tc)

                @pl.when(other)
                def _():
                    pl.semaphore_signal(
                        barrier, inc=1, device_id={"chan": z + dz, "seg": tx, "freq": tc},
                        device_id_type=MESH,
                    )

    fine_cos, fine_sin = unit_circle(0, 1, FINE, length)
    coarse_cos, coarse_sin = unit_circle(0, FINE, quarter // FINE, length)
    seeds[0] = coarse_cos
    seeds[1] = coarse_sin

    def table_rows(a, _):
        ca, sa = seeds[0, pl.ds(a, 1), :], seeds[1, pl.ds(a, 1), :]
        rows = pl.ds(pl.multiple_of(a * FINE, FINE), FINE)
        tab[rows, :BINS] = (ca * fine_cos - sa * fine_sin).astype(jnp.bfloat16)
        tab[rows, BINS:] = (-(sa * fine_cos + ca * fine_sin)).astype(jnp.bfloat16)
        return 0

    lax.fori_loop(0, quarter // FINE, table_rows, 0, unroll=4)

    live_copy.wait()
    live[...] = live_in[...].astype(jnp.float32).T
    degree = n_seg * n_freq
    up = (z > 0).astype(jnp.int32)
    down = (z < n_chan - 1).astype(jnp.int32)
    pl.semaphore_wait(barrier, degree - 1 + degree * (up + down))

    def descriptor(b, w, h):
        bb, part = b // per_granule, b % per_granule
        granule = c * gpc + bb
        below = (granule < w).astype(jnp.int32)
        tz, tx = z - below, granule - w + below * n_seg
        rows = pl.ds(pl.multiple_of(b * chunk_rows, chunk_rows), chunk_rows)
        dst_rows = pl.ds(pl.multiple_of(part * chunk_rows, chunk_rows), chunk_rows)
        src = snd.at[h, rows, :]
        dst = win.at[x, w, dst_rows, :]
        remote = pltpu.make_async_remote_copy(
            src_ref=src, dst_ref=dst, send_sem=send_sem.at[b, w, h], recv_sem=recv_sem.at[x, w, part],
            device_id={"chan": tz, "seg": tx, "freq": jnp.int32(h)}, device_id_type=MESH,
        )
        local = pltpu.make_async_copy(src, dst, recv_sem.at[x, w, part])
        mine = jnp.logical_and(jnp.logical_and(tz == z, tx == x), c == h)
        straight = jnp.logical_or(below == 0, jnp.logical_and(tz >= 0, tx == x))
        return remote, local, mine, jnp.logical_and(straight, jnp.logical_not(mine))

    half_way = per_granule // 2 if n_seg == 2 and n_freq == 2 else per_granule

    def detour(b, h):
        part = b % per_granule
        rows = pl.ds(pl.multiple_of(b * chunk_rows, chunk_rows), chunk_rows)
        slot = jnp.maximum(part - half_way, 0)
        copy = pltpu.make_async_remote_copy(
            src_ref=snd.at[h, rows, :], dst_ref=side.at[slot], send_sem=send_sem.at[b, n_seg, h],
            recv_sem=side_recv.at[slot],
            device_id={"chan": z - 1, "seg": x, "freq": jnp.int32(h)}, device_id_type=MESH,
        )
        last = c * gpc + b // per_granule == n_seg - 1
        used = jnp.logical_and(jnp.logical_and(z > 0, x == 0), jnp.logical_and(last, part >= half_way))
        return copy, used

    def onward(slot):
        rows = pl.ds((half_way + slot) * chunk_rows, chunk_rows)
        copy = pltpu.make_async_remote_copy(
            src_ref=side.at[slot], dst_ref=win.at[0, n_seg, rows, :], send_sem=side_send.at[slot],
            recv_sem=recv_sem.at[0, n_seg, half_way + slot],
            device_id={"chan": z, "seg": jnp.int32(n_seg - 1), "freq": c}, device_id_type=MESH,
        )
        return copy, jnp.logical_and(z < n_chan - 1, x == 0)

    def along_used(sx, part):
        used = jnp.logical_and(z > 0, sx != x)
        if part >= half_way and sx == 0:
            used = jnp.logical_and(used, x != n_seg - 1)
        return used

    def arrived(sx, w, part):
        dst = win.at[sx, w, pl.ds(part * chunk_rows, chunk_rows), :]
        pltpu.make_async_copy(dst, dst, recv_sem.at[sx, w, part]).wait()

    def relay(sx, w, part, to_w, tz, tx, sem):
        rows = pl.ds(part * chunk_rows, chunk_rows)
        return pltpu.make_async_remote_copy(
            src_ref=win.at[sx, w, rows, :], dst_ref=win.at[sx, to_w, rows, :], send_sem=sem,
            recv_sem=recv_sem.at[sx, to_w, part],
            device_id={"chan": tz, "seg": tx, "freq": c}, device_id_type=MESH,
        )

    def along(sx, part):
        return relay(sx, 0, part, n_seg, z - 1, x, along_sem.at[sx, part])

    def across(sx, w, tx, part):
        return relay(sx, w, part, w + x - tx, z, jnp.int32(tx), across_sem.at[sx, w - 1, tx, part])

    has_above = z < n_chan - 1

    def is_hub(sx, w):
        granule = x + w - n_seg
        own = jnp.logical_and(sx == x, jnp.logical_and(granule >= 0, granule < n_seg - 1))
        own = jnp.logical_and(own, jnp.logical_or(granule < n_seg - 2, x < n_seg - 1))
        first = jnp.logical_and(w == n_seg, jnp.logical_and(sx < x, x < n_seg - 1))
        return jnp.logical_and(has_above, jnp.logical_or(own, first))

    def hub_target(sx, w, tx):
        return jnp.logical_and(is_hub(sx, w), jnp.logical_and(tx > x + w - n_seg, tx != x))

    lane_k = 1 + lax.broadcasted_iota(jnp.int32, (1, BINS), 1)
    phase = lane_k % 4
    alpha = jnp.where(phase == 0, 1.0, jnp.where(phase == 2, -1.0, 0.0))
    beta = jnp.where(phase == 1, 1.0, jnp.where(phase == 3, -1.0, 0.0))
    sigma = jnp.where(lane_k % 2 == 0, 1.0, -1.0)

    def transform(b, _):
        for q in range(QUARTERS):
            fetch(b, q).wait()
        acc = jnp.dot(xs[b], tab[...], preferred_element_type=jnp.float32)
        part = [acc[q * chunk_rows : (q + 1) * chunk_rows] for q in range(QUARTERS)]
        re = [p[:, :BINS] for p in part]
        im = [p[:, BINS:] for p in part]
        odd_re, odd_im = re[1] + sigma * re[3], im[1] + sigma * im[3]
        full_re = re[0] + sigma * re[2] + (alpha * odd_re + beta * odd_im)
        full_im = im[0] + sigma * im[2] + (alpha * odd_im - beta * odd_re)
        energy = jnp.sum(full_re * full_re + full_im * full_im, axis=1, keepdims=True)
        scaling = lax.rsqrt(energy / (2 * BINS) + EPSILON)
        first = pl.multiple_of(z * ch_dev + c * core_ch + b * CHUNK_CH, CHUNK_CH)
        usable = live[pl.ds(first, CHUNK_CH), :]
        usable = jnp.broadcast_to(usable[:, None, :], (CHUNK_CH, segs, total_segs))
        column = lax.broadcasted_iota(jnp.int32, usable.shape, 2)
        segment = x * segs + lax.broadcasted_iota(jnp.int32, usable.shape, 1)
        usable = jnp.where(column == segment, usable, 0.0).reshape(chunk_rows, total_segs)
        usable = jnp.sum(usable, axis=1, keepdims=True)
        white_re = (full_re * scaling * usable).astype(jnp.bfloat16)
        white_im = (full_im * scaling * usable).astype(jnp.bfloat16)
        rows = pl.ds(pl.multiple_of(b * chunk_rows, chunk_rows), chunk_rows)
        for h in range(n_freq):
            snd[h, rows, :half] = white_re[:, h * half : (h + 1) * half]
            snd[h, rows, half:] = white_im[:, h * half : (h + 1) * half]
        for w in range(n_seg, -1, -1):
            for h in range(n_freq):
                remote, local, mine, other = descriptor(b, w, h)
                pl.when(other)(remote.start)
                pl.when(mine)(local.start)
        if half_way < per_granule:
            for h in range(n_freq):
                copy, used = detour(b, h)
                pl.when(used)(copy.start)
        return 0

    lax.fori_loop(0, chunks, transform, 0)

    last_block = chans // owned - 1
    for w in range(n_seg + 1):
        block = z * n_seg + x + w
        row = pl.multiple_of(jnp.minimum(block, last_block) * owned, owned)
        rows = live[pl.ds(row, owned), :]
        lv[w * owned : (w + 1) * owned, :] = jnp.where(block <= last_block, rows, 0.0)
    twice = (
        lax.broadcasted_iota(jnp.int32, (2 * OFFSETS, OFFSETS), 0) // 2
        == lax.broadcasted_iota(jnp.int32, (2 * OFFSETS, OFFSETS), 1)
    ).astype(jnp.float32).astype(jnp.bfloat16)
    ones = jnp.ones((total_segs, half), jnp.bfloat16)

    def count_pairs(i, _):
        both = (lv[pl.ds(i, OFFSETS), :] * lv[pl.ds(i, 1), :]).astype(jnp.bfloat16)
        both = jnp.dot(twice, both, preferred_element_type=jnp.float32).astype(jnp.bfloat16)
        pairs = jnp.dot(both, ones, preferred_element_type=jnp.float32)
        pairs = jnp.maximum(pairs, 1.0)
        guess = pl.reciprocal(pairs, approx=True)
        inv[i] = guess * (2.0 - pairs * guess)
        return 0

    for part in range(per_granule):
        lax.fori_loop(part * CHUNK_CH, (part + 1) * CHUNK_CH, count_pairs, 0, unroll=CHUNK_CH)
        for w in range(n_seg, 0, -1):
            for sx in range(n_seg):

                @pl.when(is_hub(sx, w))
                def _():
                    arrived(sx, w, part)
                    for tx in range(n_seg):
                        pl.when(hub_target(sx, w, tx))(across(sx, w, tx, part).start)

        for sx in range(n_seg):
            arrived(sx, 0, part)
            pl.when(along_used(sx, part))(along(sx, part).start)

        if part >= half_way:
            copy, used = onward(part - half_way)

            @pl.when(used)
            def _():
                place = side.at[part - half_way]
                pltpu.make_async_copy(place, place, side_recv.at[part - half_way]).wait()
                copy.start()

    span = n_seg * segs
    row_id = lax.broadcasted_iota(jnp.int32, (2 * KB, KB * span), 0)
    col_id = lax.broadcasted_iota(jnp.int32, (2 * KB, KB * span), 1) // span
    sum_rows = jnp.where(row_id // 2 == col_id, 1.0, 0.0).astype(jnp.bfloat16)
    real_row = lax.broadcasted_iota(jnp.int32, (2 * KB, half), 0) % 2 == 0

    sub_parts = KB // CHUNK_CH
    for t in range((n_seg + 1) * owned // KB):
        w, place = divmod(t * KB, owned)
        inside = z + (x + w) // n_seg < n_chan

        @pl.when(inside)
        def _():
            for sx in range(n_seg):
                for part in range(place // CHUNK_CH, place // CHUNK_CH + sub_parts):
                    if w > 0:
                        pl.when(jnp.logical_not(is_hub(sx, w)))(functools.partial(arrived, sx, w, part))

            def merge(m, _):
                rows = pl.ds(pl.multiple_of((place + 2 * m) * segs, 2 * segs), 2 * segs)
                parts = [win[sx, w, rows, :].astype(jnp.float32) for sx in range(n_seg)]
                for e in range(2):
                    whole = jnp.concatenate([p[e * segs : (e + 1) * segs] for p in parts], axis=0)
                    merged[t * KB + 2 * m + e] = whole.astype(jnp.bfloat16)
                return 0

            lax.fori_loop(0, KB // 2, merge, 0, unroll=4)

        @pl.when(jnp.logical_not(inside))
        def _():
            merged[t * KB : (t + 1) * KB] = jnp.zeros((KB,) + merged.shape[1:], jnp.bfloat16)

        groups = [a for a in range(owned // KB) if 0 <= t - 1 - a < OFFSETS // KB]

        def correlate(n, _):
            group = groups[0] + n // KB
            i = groups[0] * KB + n
            kb = t - 1 - group
            own = merged[i]
            other = merged[pl.ds(i + KB * kb, KB)]
            own_re, own_im = own[None, :, :half], own[None, :, half:]
            other_re, other_im = other[:, :, :half], other[:, :, half:]
            re = own_re * other_re + own_im * other_im
            im = own_re * other_im - own_im * other_re
            both = jnp.concatenate([re, im], axis=2).reshape(KB * span, 2 * half)
            total = jnp.dot(sum_rows, both, preferred_element_type=jnp.float32)
            total = jnp.where(real_row, total[:, :half], total[:, half:])
            rows = pl.ds(pl.multiple_of(2 * KB * kb, 2 * KB), 2 * KB)
            out[i, rows, :] = (total * inv[i, rows, :]).astype(jnp.bfloat16)
            return 0

        if groups:
            lax.fori_loop(0, len(groups) * KB, correlate, 0, unroll=16)

    def drain(b, _):
        for w in range(n_seg + 1):
            for h in range(n_freq):
                remote, local, mine, other = descriptor(b, w, h)
                pl.when(other)(remote.wait_send)
        if half_way < per_granule:
            for h in range(n_freq):
                copy, used = detour(b, h)
                pl.when(used)(copy.wait_send)
        return 0

    lax.fori_loop(0, chunks, drain, 0)
    for slot in range(per_granule - half_way):
        copy, used = onward(slot)
        pl.when(used)(copy.wait_send)
    for part in range(per_granule):
        for sx in range(n_seg):
            pl.when(along_used(sx, part))(along(sx, part).wait_send)
            for w in range(1, n_seg + 1):
                for tx in range(n_seg):
                    pl.when(hub_target(sx, w, tx))(across(sx, w, tx, part).wait_send)


def shards(samples, live):
    ch_dev, segs, length = samples.shape
    n_chan, n_seg, n_freq = (lax.axis_size(a) for a in ("chan", "seg", "freq"))
    owned = ch_dev // n_seg
    half = BINS // n_freq
    core_ch = ch_dev // n_freq
    chunks = core_ch // CHUNK_CH
    chunk_rows = CHUNK_CH * segs
    quarter = length // QUARTERS
    window = (n_seg + 1) * owned
    result = pl.pallas_call(
        functools.partial(kernel, n_chan, n_seg, n_freq),
        out_shape=jax.ShapeDtypeStruct((owned, 2 * OFFSETS, half), jnp.bfloat16),
        in_specs=[pl.BlockSpec(memory_space=pltpu.HBM)] * 2,
        out_specs=pl.BlockSpec(memory_space=pltpu.VMEM),
        scratch_shapes=[
            pltpu.VMEM(live.shape[::-1], jnp.int32),
            pltpu.VMEM(live.shape, jnp.float32),
            pltpu.VMEM((chunks, QUARTERS * chunk_rows, quarter), jnp.bfloat16),
            pltpu.VMEM((quarter, 2 * BINS), jnp.bfloat16),
            pltpu.VMEM((2, quarter // FINE, BINS), jnp.float32),
            pltpu.VMEM((n_freq, core_ch * segs, 2 * half), jnp.bfloat16),
            pltpu.VMEM((n_seg, n_seg + 1, owned * segs, 2 * half), jnp.bfloat16),
            pltpu.VMEM((window, n_seg * segs, 2 * half), jnp.bfloat16),
            pltpu.VMEM((window, n_seg * segs), jnp.float32),
            pltpu.VMEM((owned, 2 * OFFSETS, half), jnp.float32),
            pltpu.SemaphoreType.DMA,
            pltpu.SemaphoreType.DMA((chunks, QUARTERS)),
            pltpu.SemaphoreType.DMA((chunks, n_seg + 1, n_freq)),
            pltpu.SemaphoreType.DMA((n_seg, n_seg + 1, owned // CHUNK_CH)),
            pltpu.SemaphoreType.DMA((n_seg, owned // CHUNK_CH)),
            pltpu.SemaphoreType.DMA((n_seg, n_seg, n_seg, owned // CHUNK_CH)),
            pltpu.VMEM((owned // CHUNK_CH, chunk_rows, 2 * half), jnp.bfloat16),
            pltpu.SemaphoreType.DMA((owned // CHUNK_CH,)),
            pltpu.SemaphoreType.DMA((owned // CHUNK_CH,)),
        ],
        compiler_params=pltpu.CompilerParams(
            collective_id=0, has_side_effects=True, vmem_limit_bytes=48 * 1024 * 1024
        ),
    )(samples.reshape(ch_dev * segs, length), live.T)
    return result.reshape(owned, OFFSETS, 2, half)


def solution(mesh):
    return jax.shard_map(
        shards,
        mesh=mesh,
        in_specs=(P(("cable", "chan"), "seg", None), P("cable", None)),
        out_specs=P(("cable", "chan", "seg"), None, None, "freq"),
        check_vma=False,
    )
```

```python
import functools
import math

import jax
import jax.numpy as jnp
from jax import lax
from jax.experimental import pallas as pl
from jax.experimental.pallas import tpu as pltpu
from jax.sharding import PartitionSpec as P

BINS = 256
OFFSETS = 64
EPSILON = 1e-06
QUARTERS = 4
FINE = 64
CHUNK_CH = 8
KB = 16
MESH = pl.DeviceIdType.MESH


def unit_circle(first, step, count, length):
    t = first + step * lax.broadcasted_iota(jnp.int32, (count, BINS), 0)
    k = 1 + lax.broadcasted_iota(jnp.int32, (count, BINS), 1)
    m = lax.rem(t * k, length)
    m = jnp.where(m >= length // 2, m - length, m)
    y = m.astype(jnp.float32) * (math.pi / length)
    y2 = y * y
    sine = jnp.full_like(y, 1.0 / math.factorial(13))
    for order in (11, 9, 7, 5, 3, 1):
        sine = sine * y2 + (-1.0) ** (order // 2) / math.factorial(order)
    sine = sine * y
    cosine = jnp.full_like(y, -1.0 / math.factorial(14))
    for order in (12, 10, 8, 6, 4, 2, 0):
        cosine = cosine * y2 + (-1.0) ** (order // 2) / math.factorial(order)
    return 1.0 - 2.0 * sine * sine, 2.0 * sine * cosine


def kernel(
    n_chan, n_seg, n_freq, samples, live_hbm, out, live_in, live, xs, tab, seeds, snd, win, merged, lv, inv,
    live_sem, x_sem, send_sem, recv_sem, along_sem, across_sem,
    side, side_recv, side_send,
):
    length = samples.shape[1]
    quarter = length // QUARTERS
    total_segs, chans = live_in.shape
    ch_dev = chans // n_chan
    segs = samples.shape[0] // ch_dev
    owned = ch_dev // n_seg
    half = BINS // n_freq
    core_ch = ch_dev // n_freq
    gpc = n_seg // n_freq
    chunk_rows = CHUNK_CH * segs
    chunks = core_ch // CHUNK_CH
    per_granule = owned // CHUNK_CH
    z, x, c = lax.axis_index("chan"), lax.axis_index("seg"), lax.axis_index("freq")

    def fetch(b, q):
        row = pl.multiple_of((c * chunks + b) * chunk_rows, chunk_rows)
        return pltpu.make_async_copy(
            samples.at[pl.ds(row, chunk_rows), pl.ds(q * quarter, quarter)],
            xs.at[b, pl.ds(q * chunk_rows, chunk_rows), :],
            x_sem.at[b, q],
        )

    for b in range(chunks):
        for q in range(QUARTERS):
            fetch(b, q).start()
    live_copy = pltpu.make_async_copy(live_hbm, live_in, live_sem)
    live_copy.start()

    barrier = pltpu.get_barrier_semaphore()
    for dz in (-1, 0, 1):
        near = jnp.logical_and(z + dz >= 0, z + dz < n_chan)
        for tx in range(n_seg):
            for tc in range(n_freq):
                other = near if dz else jnp.logical_or(x != tx, c != tc)

                @pl.when(other)
                def _():
                    pl.semaphore_signal(
                        barrier, inc=1, device_id={"chan": z + dz, "seg": tx, "freq": tc},
                        device_id_type=MESH,
                    )

    fine_cos, fine_sin = unit_circle(0, 1, FINE, length)
    coarse_cos, coarse_sin = unit_circle(0, FINE, quarter // FINE, length)
    seeds[0] = coarse_cos
    seeds[1] = coarse_sin

    def table_rows(a, _):
        ca, sa = seeds[0, pl.ds(a, 1), :], seeds[1, pl.ds(a, 1), :]
        rows = pl.ds(pl.multiple_of(a * FINE, FINE), FINE)
        tab[rows, :BINS] = (ca * fine_cos - sa * fine_sin).astype(jnp.bfloat16)
        tab[rows, BINS:] = (-(sa * fine_cos + ca * fine_sin)).astype(jnp.bfloat16)
        return 0

    lax.fori_loop(0, quarter // FINE, table_rows, 0, unroll=4)

    live_copy.wait()
    live[...] = live_in[...].astype(jnp.float32).T
    degree = n_seg * n_freq
    up = (z > 0).astype(jnp.int32)
    down = (z < n_chan - 1).astype(jnp.int32)
    pl.semaphore_wait(barrier, degree - 1 + degree * (up + down))

    def descriptor(b, w, h):
        bb, part = b // per_granule, b % per_granule
        granule = c * gpc + bb
        below = (granule < w).astype(jnp.int32)
        tz, tx = z - below, granule - w + below * n_seg
        rows = pl.ds(pl.multiple_of(b * chunk_rows, chunk_rows), chunk_rows)
        dst_rows = pl.ds(pl.multiple_of(part * chunk_rows, chunk_rows), chunk_rows)
        src = snd.at[h, rows, :]
        dst = win.at[x, w, dst_rows, :]
        remote = pltpu.make_async_remote_copy(
            src_ref=src, dst_ref=dst, send_sem=send_sem.at[b, w, h], recv_sem=recv_sem.at[x, w, part],
            device_id={"chan": tz, "seg": tx, "freq": jnp.int32(h)}, device_id_type=MESH,
        )
        local = pltpu.make_async_copy(src, dst, recv_sem.at[x, w, part])
        mine = jnp.logical_and(jnp.logical_and(tz == z, tx == x), c == h)
        straight = jnp.logical_or(below == 0, jnp.logical_and(tz >= 0, tx == x))
        return remote, local, mine, jnp.logical_and(straight, jnp.logical_not(mine))

    half_way = per_granule // 2 if n_seg == 2 and n_freq == 2 else per_granule

    def detour(b, h):
        part = b % per_granule
        rows = pl.ds(pl.multiple_of(b * chunk_rows, chunk_rows), chunk_rows)
        slot = jnp.maximum(part - half_way, 0)
        copy = pltpu.make_async_remote_copy(
            src_ref=snd.at[h, rows, :], dst_ref=side.at[slot], send_sem=send_sem.at[b, n_seg, h],
            recv_sem=side_recv.at[slot],
            device_id={"chan": z - 1, "seg": x, "freq": jnp.int32(h)}, device_id_type=MESH,
        )
        last = c * gpc + b // per_granule == n_seg - 1
        used = jnp.logical_and(jnp.logical_and(z > 0, x == 0), jnp.logical_and(last, part >= half_way))
        return copy, used

    def onward(slot):
        rows = pl.ds((half_way + slot) * chunk_rows, chunk_rows)
        copy = pltpu.make_async_remote_copy(
            src_ref=side.at[slot], dst_ref=win.at[0, n_seg, rows, :], send_sem=side_send.at[slot],
            recv_sem=recv_sem.at[0, n_seg, half_way + slot],
            device_id={"chan": z, "seg": jnp.int32(n_seg - 1), "freq": c}, device_id_type=MESH,
        )
        return copy, jnp.logical_and(z < n_chan - 1, x == 0)

    def along_used(sx, part):
        used = jnp.logical_and(z > 0, sx != x)
        if part >= half_way and sx == 0:
            used = jnp.logical_and(used, x != n_seg - 1)
        return used

    def arrived(sx, w, part):
        dst = win.at[sx, w, pl.ds(part * chunk_rows, chunk_rows), :]
        pltpu.make_async_copy(dst, dst, recv_sem.at[sx, w, part]).wait()

    def relay(sx, w, part, to_w, tz, tx, sem):
        rows = pl.ds(part * chunk_rows, chunk_rows)
        return pltpu.make_async_remote_copy(
            src_ref=win.at[sx, w, rows, :], dst_ref=win.at[sx, to_w, rows, :], send_sem=sem,
            recv_sem=recv_sem.at[sx, to_w, part],
            device_id={"chan": tz, "seg": tx, "freq": c}, device_id_type=MESH,
        )

    def along(sx, part):
        return relay(sx, 0, part, n_seg, z - 1, x, along_sem.at[sx, part])

    def across(sx, w, tx, part):
        return relay(sx, w, part, w + x - tx, z, jnp.int32(tx), across_sem.at[sx, w - 1, tx, part])

    has_above = z < n_chan - 1

    def is_hub(sx, w):
        granule = x + w - n_seg
        own = jnp.logical_and(sx == x, jnp.logical_and(granule >= 0, granule < n_seg - 1))
        own = jnp.logical_and(own, jnp.logical_or(granule < n_seg - 2, x < n_seg - 1))
        first = jnp.logical_and(w == n_seg, jnp.logical_and(sx < x, x < n_seg - 1))
        return jnp.logical_and(has_above, jnp.logical_or(own, first))

    def hub_target(sx, w, tx):
        return jnp.logical_and(is_hub(sx, w), jnp.logical_and(tx > x + w - n_seg, tx != x))

    lane_k = 1 + lax.broadcasted_iota(jnp.int32, (1, BINS), 1)
    phase = lane_k % 4
    alpha = jnp.where(phase == 0, 1.0, jnp.where(phase == 2, -1.0, 0.0))
    beta = jnp.where(phase == 1, 1.0, jnp.where(phase == 3, -1.0, 0.0))
    sigma = jnp.where(lane_k % 2 == 0, 1.0, -1.0)

    def send_late(b):
        later = c * gpc + b // per_granule > 0
        for w in range(n_seg, 0, -1):
            for h in range(n_freq):
                remote, local, mine, other = descriptor(b, w, h)
                pl.when(jnp.logical_and(other, later))(remote.start)
        if half_way < per_granule:
            for h in range(n_freq):
                copy, used = detour(b, h)
                pl.when(used)(copy.start)

    def transform(b, _):
        for q in range(QUARTERS):
            fetch(b, q).wait()
        acc = jnp.dot(xs[b], tab[...], preferred_element_type=jnp.float32)
        part = [acc[q * chunk_rows : (q + 1) * chunk_rows] for q in range(QUARTERS)]
        re = [p[:, :BINS] for p in part]
        im = [p[:, BINS:] for p in part]
        odd_re, odd_im = re[1] + sigma * re[3], im[1] + sigma * im[3]
        full_re = re[0] + sigma * re[2] + (alpha * odd_re + beta * odd_im)
        full_im = im[0] + sigma * im[2] + (alpha * odd_im - beta * odd_re)
        energy = jnp.sum(full_re * full_re + full_im * full_im, axis=1, keepdims=True)
        scaling = lax.rsqrt(energy / (2 * BINS) + EPSILON)
        first = pl.multiple_of(z * ch_dev + c * core_ch + b * CHUNK_CH, CHUNK_CH)
        usable = live[pl.ds(first, CHUNK_CH), :]
        usable = jnp.broadcast_to(usable[:, None, :], (CHUNK_CH, segs, total_segs))
        column = lax.broadcasted_iota(jnp.int32, usable.shape, 2)
        segment = x * segs + lax.broadcasted_iota(jnp.int32, usable.shape, 1)
        usable = jnp.where(column == segment, usable, 0.0).reshape(chunk_rows, total_segs)
        usable = jnp.sum(usable, axis=1, keepdims=True)
        white_re = (full_re * scaling * usable).astype(jnp.bfloat16)
        white_im = (full_im * scaling * usable).astype(jnp.bfloat16)
        rows = pl.ds(pl.multiple_of(b * chunk_rows, chunk_rows), chunk_rows)
        for h in range(n_freq):
            snd[h, rows, :half] = white_re[:, h * half : (h + 1) * half]
            snd[h, rows, half:] = white_im[:, h * half : (h + 1) * half]
        first_granule = c * gpc + b // per_granule == 0
        for w in range(n_seg, -1, -1):
            for h in range(n_freq):
                remote, local, mine, other = descriptor(b, w, h)
                soon = other if w == 0 else jnp.logical_and(other, first_granule)
                pl.when(soon)(remote.start)
                pl.when(mine)(local.start)
        pl.when(b > 0)(functools.partial(send_late, b - 1))
        return 0

    lax.fori_loop(0, chunks, transform, 0)
    send_late(jnp.int32(chunks - 1))

    last_block = chans // owned - 1
    for w in range(n_seg + 1):
        block = z * n_seg + x + w
        row = pl.multiple_of(jnp.minimum(block, last_block) * owned, owned)
        rows = live[pl.ds(row, owned), :]
        lv[w * owned : (w + 1) * owned, :] = jnp.where(block <= last_block, rows, 0.0)
    twice = (
        lax.broadcasted_iota(jnp.int32, (2 * OFFSETS, OFFSETS), 0) // 2
        == lax.broadcasted_iota(jnp.int32, (2 * OFFSETS, OFFSETS), 1)
    ).astype(jnp.float32).astype(jnp.bfloat16)
    ones = jnp.ones((total_segs, half), jnp.bfloat16)

    def count_pairs(i, _):
        both = (lv[pl.ds(i, OFFSETS), :] * lv[pl.ds(i, 1), :]).astype(jnp.bfloat16)
        both = jnp.dot(twice, both, preferred_element_type=jnp.float32).astype(jnp.bfloat16)
        pairs = jnp.dot(both, ones, preferred_element_type=jnp.float32)
        pairs = jnp.maximum(pairs, 1.0)
        guess = pl.reciprocal(pairs, approx=True)
        inv[i] = guess * (2.0 - pairs * guess)
        return 0

    for part in range(per_granule):
        lax.fori_loop(part * CHUNK_CH, (part + 1) * CHUNK_CH, count_pairs, 0, unroll=CHUNK_CH)
        for w in range(n_seg, 0, -1):
            for sx in range(n_seg):

                @pl.when(is_hub(sx, w))
                def _():
                    arrived(sx, w, part)
                    for tx in range(n_seg):
                        pl.when(hub_target(sx, w, tx))(across(sx, w, tx, part).start)

        for sx in range(n_seg):
            arrived(sx, 0, part)
            pl.when(along_used(sx, part))(along(sx, part).start)

        if part >= half_way:
            copy, used = onward(part - half_way)

            @pl.when(used)
            def _():
                place = side.at[part - half_way]
                pltpu.make_async_copy(place, place, side_recv.at[part - half_way]).wait()
                copy.start()

    span = n_seg * segs
    row_id = lax.broadcasted_iota(jnp.int32, (2 * KB, KB * span), 0)
    col_id = lax.broadcasted_iota(jnp.int32, (2 * KB, KB * span), 1) // span
    sum_rows = jnp.where(row_id // 2 == col_id, 1.0, 0.0).astype(jnp.bfloat16)
    real_row = lax.broadcasted_iota(jnp.int32, (2 * KB, half), 0) % 2 == 0

    sub_parts = KB // CHUNK_CH
    for t in range((n_seg + 1) * owned // KB):
        w, place = divmod(t * KB, owned)
        inside = z + (x + w) // n_seg < n_chan

        @pl.when(inside)
        def _():
            for sx in range(n_seg):
                for part in range(place // CHUNK_CH, place // CHUNK_CH + sub_parts):
                    if w > 0:
                        pl.when(jnp.logical_not(is_hub(sx, w)))(functools.partial(arrived, sx, w, part))

            def merge(m, _):
                rows = pl.ds(pl.multiple_of((place + 2 * m) * segs, 2 * segs), 2 * segs)
                parts = [win[sx, w, rows, :].astype(jnp.float32) for sx in range(n_seg)]
                for e in range(2):
                    whole = jnp.concatenate([p[e * segs : (e + 1) * segs] for p in parts], axis=0)
                    merged[t * KB + 2 * m + e] = whole.astype(jnp.bfloat16)
                return 0

            lax.fori_loop(0, KB // 2, merge, 0, unroll=4)

        @pl.when(jnp.logical_not(inside))
        def _():
            merged[t * KB : (t + 1) * KB] = jnp.zeros((KB,) + merged.shape[1:], jnp.bfloat16)

        groups = [a for a in range(owned // KB) if 0 <= t - 1 - a < OFFSETS // KB]

        def correlate(n, _):
            group = groups[0] + n // KB
            i = groups[0] * KB + n
            kb = t - 1 - group
            own = merged[i]
            other = merged[pl.ds(i + KB * kb, KB)]
            own_re, own_im = own[None, :, :half], own[None, :, half:]
            other_re, other_im = other[:, :, :half], other[:, :, half:]
            re = own_re * other_re + own_im * other_im
            im = own_re * other_im - own_im * other_re
            both = jnp.concatenate([re, im], axis=2).reshape(KB * span, 2 * half)
            total = jnp.dot(sum_rows, both, preferred_element_type=jnp.float32)
            total = jnp.where(real_row, total[:, :half], total[:, half:])
            rows = pl.ds(pl.multiple_of(2 * KB * kb, 2 * KB), 2 * KB)
            out[i, rows, :] = (total * inv[i, rows, :]).astype(jnp.bfloat16)
            return 0

        if groups:
            lax.fori_loop(0, len(groups) * KB, correlate, 0, unroll=16)

    def drain(b, _):
        for w in range(n_seg + 1):
            for h in range(n_freq):
                remote, local, mine, other = descriptor(b, w, h)
                pl.when(other)(remote.wait_send)
        if half_way < per_granule:
            for h in range(n_freq):
                copy, used = detour(b, h)
                pl.when(used)(copy.wait_send)
        return 0

    lax.fori_loop(0, chunks, drain, 0)
    for slot in range(per_granule - half_way):
        copy, used = onward(slot)
        pl.when(used)(copy.wait_send)
    for part in range(per_granule):
        for sx in range(n_seg):
            pl.when(along_used(sx, part))(along(sx, part).wait_send)
            for w in range(1, n_seg + 1):
                for tx in range(n_seg):
                    pl.when(hub_target(sx, w, tx))(across(sx, w, tx, part).wait_send)


def shards(samples, live):
    ch_dev, segs, length = samples.shape
    n_chan, n_seg, n_freq = (lax.axis_size(a) for a in ("chan", "seg", "freq"))
    owned = ch_dev // n_seg
    half = BINS // n_freq
    core_ch = ch_dev // n_freq
    chunks = core_ch // CHUNK_CH
    chunk_rows = CHUNK_CH * segs
    quarter = length // QUARTERS
    window = (n_seg + 1) * owned
    result = pl.pallas_call(
        functools.partial(kernel, n_chan, n_seg, n_freq),
        out_shape=jax.ShapeDtypeStruct((owned, 2 * OFFSETS, half), jnp.bfloat16),
        in_specs=[pl.BlockSpec(memory_space=pltpu.HBM)] * 2,
        out_specs=pl.BlockSpec(memory_space=pltpu.VMEM),
        scratch_shapes=[
            pltpu.VMEM(live.shape[::-1], jnp.int32),
            pltpu.VMEM(live.shape, jnp.float32),
            pltpu.VMEM((chunks, QUARTERS * chunk_rows, quarter), jnp.bfloat16),
            pltpu.VMEM((quarter, 2 * BINS), jnp.bfloat16),
            pltpu.VMEM((2, quarter // FINE, BINS), jnp.float32),
            pltpu.VMEM((n_freq, core_ch * segs, 2 * half), jnp.bfloat16),
            pltpu.VMEM((n_seg, n_seg + 1, owned * segs, 2 * half), jnp.bfloat16),
            pltpu.VMEM((window, n_seg * segs, 2 * half), jnp.bfloat16),
            pltpu.VMEM((window, n_seg * segs), jnp.float32),
            pltpu.VMEM((owned, 2 * OFFSETS, half), jnp.float32),
            pltpu.SemaphoreType.DMA,
            pltpu.SemaphoreType.DMA((chunks, QUARTERS)),
            pltpu.SemaphoreType.DMA((chunks, n_seg + 1, n_freq)),
            pltpu.SemaphoreType.DMA((n_seg, n_seg + 1, owned // CHUNK_CH)),
            pltpu.SemaphoreType.DMA((n_seg, owned // CHUNK_CH)),
            pltpu.SemaphoreType.DMA((n_seg, n_seg, n_seg, owned // CHUNK_CH)),
            pltpu.VMEM((owned // CHUNK_CH, chunk_rows, 2 * half), jnp.bfloat16),
            pltpu.SemaphoreType.DMA((owned // CHUNK_CH,)),
            pltpu.SemaphoreType.DMA((owned // CHUNK_CH,)),
        ],
        compiler_params=pltpu.CompilerParams(
            collective_id=0, has_side_effects=True, vmem_limit_bytes=48 * 1024 * 1024
        ),
    )(samples.reshape(ch_dev * segs, length), live.T)
    return result.reshape(owned, OFFSETS, 2, half)


def solution(mesh):
    return jax.shard_map(
        shards,
        mesh=mesh,
        in_specs=(P(("cable", "chan"), "seg", None), P("cable", None)),
        out_specs=P(("cable", "chan", "seg"), None, None, "freq"),
        check_vma=False,
    )
```

```python
import functools
import math

import jax
import jax.numpy as jnp
from jax import lax
from jax.experimental import pallas as pl
from jax.experimental.pallas import tpu as pltpu
from jax.sharding import PartitionSpec as P

BINS = 256
OFFSETS = 64
EPSILON = 1e-06
QUARTERS = 4
FINE = 64
CHUNK_CH = 8
KB = 16
MESH = pl.DeviceIdType.MESH


def unit_circle(first, step, count, length):
    t = first + step * lax.broadcasted_iota(jnp.int32, (count, BINS), 0)
    k = 1 + lax.broadcasted_iota(jnp.int32, (count, BINS), 1)
    m = lax.rem(t * k, length)
    m = jnp.where(m >= length // 2, m - length, m)
    y = m.astype(jnp.float32) * (math.pi / length)
    y2 = y * y
    sine = jnp.full_like(y, 1.0 / math.factorial(13))
    for order in (11, 9, 7, 5, 3, 1):
        sine = sine * y2 + (-1.0) ** (order // 2) / math.factorial(order)
    sine = sine * y
    cosine = jnp.full_like(y, -1.0 / math.factorial(14))
    for order in (12, 10, 8, 6, 4, 2, 0):
        cosine = cosine * y2 + (-1.0) ** (order // 2) / math.factorial(order)
    return 1.0 - 2.0 * sine * sine, 2.0 * sine * cosine


def kernel(
    n_chan, n_seg, n_freq, samples, live_hbm, out, live_in, live, xs, tab, seeds, snd, win, merged, lv, inv,
    live_sem, x_sem, send_sem, recv_sem, along_sem, across_sem,
    side, side_recv, side_send,
):
    length = samples.shape[1]
    quarter = length // QUARTERS
    total_segs, chans = live_in.shape
    ch_dev = chans // n_chan
    segs = samples.shape[0] // ch_dev
    owned = ch_dev // n_seg
    half = BINS // n_freq
    core_ch = ch_dev // n_freq
    gpc = n_seg // n_freq
    chunk_rows = CHUNK_CH * segs
    chunks = core_ch // CHUNK_CH
    per_granule = owned // CHUNK_CH
    z, x, c = lax.axis_index("chan"), lax.axis_index("seg"), lax.axis_index("freq")

    def fetch(b, q):
        row = pl.multiple_of((c * chunks + b) * chunk_rows, chunk_rows)
        return pltpu.make_async_copy(
            samples.at[pl.ds(row, chunk_rows), pl.ds(q * quarter, quarter)],
            xs.at[b, pl.ds(q * chunk_rows, chunk_rows), :],
            x_sem.at[b, q],
        )

    for b in range(chunks):
        for q in range(QUARTERS):
            fetch(b, q).start()
    live_copy = pltpu.make_async_copy(live_hbm, live_in, live_sem)
    live_copy.start()

    barrier = pltpu.get_barrier_semaphore()
    for dz in (-1, 0, 1):
        near = jnp.logical_and(z + dz >= 0, z + dz < n_chan)
        for tx in range(n_seg):
            for tc in range(n_freq):
                other = near if dz else jnp.logical_or(x != tx, c != tc)

                @pl.when(other)
                def _():
                    pl.semaphore_signal(
                        barrier, inc=1, device_id={"chan": z + dz, "seg": tx, "freq": tc},
                        device_id_type=MESH,
                    )

    fine_cos, fine_sin = unit_circle(0, 1, FINE, length)
    coarse_cos, coarse_sin = unit_circle(0, FINE, quarter // FINE, length)
    seeds[0] = coarse_cos
    seeds[1] = coarse_sin

    def table_rows(a, _):
        ca, sa = seeds[0, pl.ds(a, 1), :], seeds[1, pl.ds(a, 1), :]
        rows = pl.ds(pl.multiple_of(a * FINE, FINE), FINE)
        tab[rows, :BINS] = (ca * fine_cos - sa * fine_sin).astype(jnp.bfloat16)
        tab[rows, BINS:] = (-(sa * fine_cos + ca * fine_sin)).astype(jnp.bfloat16)
        return 0

    lax.fori_loop(0, quarter // FINE, table_rows, 0, unroll=4)

    live_copy.wait()
    live[...] = live_in[...].astype(jnp.float32).T
    degree = n_seg * n_freq
    up = (z > 0).astype(jnp.int32)
    down = (z < n_chan - 1).astype(jnp.int32)
    pl.semaphore_wait(barrier, degree - 1 + degree * (up + down))

    def descriptor(b, w, h):
        bb, part = b // per_granule, b % per_granule
        granule = c * gpc + bb
        below = (granule < w).astype(jnp.int32)
        tz, tx = z - below, granule - w + below * n_seg
        rows = pl.ds(pl.multiple_of(b * chunk_rows, chunk_rows), chunk_rows)
        dst_rows = pl.ds(pl.multiple_of(part * chunk_rows, chunk_rows), chunk_rows)
        src = snd.at[h, rows, :]
        dst = win.at[x, w, dst_rows, :]
        remote = pltpu.make_async_remote_copy(
            src_ref=src, dst_ref=dst, send_sem=send_sem.at[b, w, h], recv_sem=recv_sem.at[x, w, part],
            device_id={"chan": tz, "seg": tx, "freq": jnp.int32(h)}, device_id_type=MESH,
        )
        local = pltpu.make_async_copy(src, dst, recv_sem.at[x, w, part])
        mine = jnp.logical_and(jnp.logical_and(tz == z, tx == x), c == h)
        straight = jnp.logical_or(below == 0, jnp.logical_and(tz >= 0, tx == x))
        return remote, local, mine, jnp.logical_and(straight, jnp.logical_not(mine))

    half_way = per_granule // 2 if n_seg == 2 and n_freq == 2 else per_granule

    def detour(b, h):
        part = b % per_granule
        rows = pl.ds(pl.multiple_of(b * chunk_rows, chunk_rows), chunk_rows)
        slot = jnp.maximum(part - half_way, 0)
        copy = pltpu.make_async_remote_copy(
            src_ref=snd.at[h, rows, :], dst_ref=side.at[slot], send_sem=send_sem.at[b, n_seg, h],
            recv_sem=side_recv.at[slot],
            device_id={"chan": z - 1, "seg": x, "freq": jnp.int32(h)}, device_id_type=MESH,
        )
        last = c * gpc + b // per_granule == n_seg - 1
        used = jnp.logical_and(jnp.logical_and(z > 0, x == 0), jnp.logical_and(last, part >= half_way))
        return copy, used

    def onward(slot):
        rows = pl.ds((half_way + slot) * chunk_rows, chunk_rows)
        copy = pltpu.make_async_remote_copy(
            src_ref=side.at[slot], dst_ref=win.at[0, n_seg, rows, :], send_sem=side_send.at[slot],
            recv_sem=recv_sem.at[0, n_seg, half_way + slot],
            device_id={"chan": z, "seg": jnp.int32(n_seg - 1), "freq": c}, device_id_type=MESH,
        )
        return copy, jnp.logical_and(z < n_chan - 1, x == 0)

    def along_used(sx, part):
        used = jnp.logical_and(z > 0, sx != x)
        if part >= half_way and sx == 0:
            used = jnp.logical_and(used, x != n_seg - 1)
        return used

    def arrived(sx, w, part):
        dst = win.at[sx, w, pl.ds(part * chunk_rows, chunk_rows), :]
        pltpu.make_async_copy(dst, dst, recv_sem.at[sx, w, part]).wait()

    def relay(sx, w, part, to_w, tz, tx, sem):
        rows = pl.ds(part * chunk_rows, chunk_rows)
        return pltpu.make_async_remote_copy(
            src_ref=win.at[sx, w, rows, :], dst_ref=win.at[sx, to_w, rows, :], send_sem=sem,
            recv_sem=recv_sem.at[sx, to_w, part],
            device_id={"chan": tz, "seg": tx, "freq": c}, device_id_type=MESH,
        )

    def along(sx, part):
        return relay(sx, 0, part, n_seg, z - 1, x, along_sem.at[sx, part])

    def across(sx, w, tx, part):
        return relay(sx, w, part, w + x - tx, z, jnp.int32(tx), across_sem.at[sx, w - 1, tx, part])

    has_above = z < n_chan - 1

    def is_hub(sx, w):
        granule = x + w - n_seg
        own = jnp.logical_and(sx == x, jnp.logical_and(granule >= 0, granule < n_seg - 1))
        own = jnp.logical_and(own, jnp.logical_or(granule < n_seg - 2, x < n_seg - 1))
        first = jnp.logical_and(w == n_seg, jnp.logical_and(sx < x, x < n_seg - 1))
        return jnp.logical_and(has_above, jnp.logical_or(own, first))

    def hub_target(sx, w, tx):
        return jnp.logical_and(is_hub(sx, w), jnp.logical_and(tx > x + w - n_seg, tx != x))

    lane_k = 1 + lax.broadcasted_iota(jnp.int32, (1, BINS), 1)
    phase = lane_k % 4
    alpha = jnp.where(phase == 0, 1.0, jnp.where(phase == 2, -1.0, 0.0))
    beta = jnp.where(phase == 1, 1.0, jnp.where(phase == 3, -1.0, 0.0))
    sigma = jnp.where(lane_k % 2 == 0, 1.0, -1.0)

    def send_late(b):
        granule = c * gpc + b // per_granule
        for w in range(n_seg, 0, -1):
            for h in range(n_freq):
                remote, local, mine, other = descriptor(b, w, h)
                later = jnp.logical_and(granule > 0, granule < w)
                pl.when(jnp.logical_and(other, later))(remote.start)
        if half_way < per_granule:
            for h in range(n_freq):
                copy, used = detour(b, h)
                pl.when(used)(copy.start)

    def transform(b, _):
        for q in range(QUARTERS):
            fetch(b, q).wait()
        acc = jnp.dot(xs[b], tab[...], preferred_element_type=jnp.float32)
        part = [acc[q * chunk_rows : (q + 1) * chunk_rows] for q in range(QUARTERS)]
        re = [p[:, :BINS] for p in part]
        im = [p[:, BINS:] for p in part]
        odd_re, odd_im = re[1] + sigma * re[3], im[1] + sigma * im[3]
        full_re = re[0] + sigma * re[2] + (alpha * odd_re + beta * odd_im)
        full_im = im[0] + sigma * im[2] + (alpha * odd_im - beta * odd_re)
        energy = jnp.sum(full_re * full_re + full_im * full_im, axis=1, keepdims=True)
        scaling = lax.rsqrt(energy / (2 * BINS) + EPSILON)
        first = pl.multiple_of(z * ch_dev + c * core_ch + b * CHUNK_CH, CHUNK_CH)
        usable = live[pl.ds(first, CHUNK_CH), :]
        usable = jnp.broadcast_to(usable[:, None, :], (CHUNK_CH, segs, total_segs))
        column = lax.broadcasted_iota(jnp.int32, usable.shape, 2)
        segment = x * segs + lax.broadcasted_iota(jnp.int32, usable.shape, 1)
        usable = jnp.where(column == segment, usable, 0.0).reshape(chunk_rows, total_segs)
        usable = jnp.sum(usable, axis=1, keepdims=True)
        white_re = (full_re * scaling * usable).astype(jnp.bfloat16)
        white_im = (full_im * scaling * usable).astype(jnp.bfloat16)
        rows = pl.ds(pl.multiple_of(b * chunk_rows, chunk_rows), chunk_rows)
        for h in range(n_freq):
            snd[h, rows, :half] = white_re[:, h * half : (h + 1) * half]
            snd[h, rows, half:] = white_im[:, h * half : (h + 1) * half]
        granule = c * gpc + b // per_granule
        for w in range(n_seg, -1, -1):
            for h in range(n_freq):
                remote, local, mine, other = descriptor(b, w, h)
                at_once = jnp.logical_or(granule == 0, granule >= w)
                soon = jnp.logical_and(other, at_once)
                pl.when(soon)(remote.start)
                pl.when(mine)(local.start)
        pl.when(b > 0)(functools.partial(send_late, b - 1))
        return 0

    lax.fori_loop(0, chunks, transform, 0)
    send_late(jnp.int32(chunks - 1))

    last_block = chans // owned - 1
    for w in range(n_seg + 1):
        block = z * n_seg + x + w
        row = pl.multiple_of(jnp.minimum(block, last_block) * owned, owned)
        rows = live[pl.ds(row, owned), :]
        lv[w * owned : (w + 1) * owned, :] = jnp.where(block <= last_block, rows, 0.0)
    twice = (
        lax.broadcasted_iota(jnp.int32, (2 * OFFSETS, OFFSETS), 0) // 2
        == lax.broadcasted_iota(jnp.int32, (2 * OFFSETS, OFFSETS), 1)
    ).astype(jnp.float32).astype(jnp.bfloat16)
    ones = jnp.ones((total_segs, half), jnp.bfloat16)

    def count_pairs(i, _):
        both = (lv[pl.ds(i, OFFSETS), :] * lv[pl.ds(i, 1), :]).astype(jnp.bfloat16)
        both = jnp.dot(twice, both, preferred_element_type=jnp.float32).astype(jnp.bfloat16)
        pairs = jnp.dot(both, ones, preferred_element_type=jnp.float32)
        pairs = jnp.maximum(pairs, 1.0)
        guess = pl.reciprocal(pairs, approx=True)
        inv[i] = guess * (2.0 - pairs * guess)
        return 0

    for part in range(per_granule):
        lax.fori_loop(part * CHUNK_CH, (part + 1) * CHUNK_CH, count_pairs, 0, unroll=CHUNK_CH)
        for w in range(n_seg, 0, -1):
            for sx in range(n_seg):

                @pl.when(is_hub(sx, w))
                def _():
                    arrived(sx, w, part)
                    for tx in range(n_seg):
                        pl.when(hub_target(sx, w, tx))(across(sx, w, tx, part).start)

        for sx in range(n_seg):
            arrived(sx, 0, part)
            pl.when(along_used(sx, part))(along(sx, part).start)

        if part >= half_way:
            copy, used = onward(part - half_way)

            @pl.when(used)
            def _():
                place = side.at[part - half_way]
                pltpu.make_async_copy(place, place, side_recv.at[part - half_way]).wait()
                copy.start()

    span = n_seg * segs
    row_id = lax.broadcasted_iota(jnp.int32, (2 * KB, KB * span), 0)
    col_id = lax.broadcasted_iota(jnp.int32, (2 * KB, KB * span), 1) // span
    sum_rows = jnp.where(row_id // 2 == col_id, 1.0, 0.0).astype(jnp.bfloat16)
    real_row = lax.broadcasted_iota(jnp.int32, (2 * KB, half), 0) % 2 == 0

    sub_parts = KB // CHUNK_CH
    for t in range((n_seg + 1) * owned // KB):
        w, place = divmod(t * KB, owned)
        inside = z + (x + w) // n_seg < n_chan

        @pl.when(inside)
        def _():
            for sx in range(n_seg):
                for part in range(place // CHUNK_CH, place // CHUNK_CH + sub_parts):
                    if w > 0:
                        pl.when(jnp.logical_not(is_hub(sx, w)))(functools.partial(arrived, sx, w, part))

            def merge(m, _):
                rows = pl.ds(pl.multiple_of((place + 2 * m) * segs, 2 * segs), 2 * segs)
                parts = [win[sx, w, rows, :].astype(jnp.float32) for sx in range(n_seg)]
                for e in range(2):
                    whole = jnp.concatenate([p[e * segs : (e + 1) * segs] for p in parts], axis=0)
                    merged[t * KB + 2 * m + e] = whole.astype(jnp.bfloat16)
                return 0

            lax.fori_loop(0, KB // 2, merge, 0, unroll=4)

        @pl.when(jnp.logical_not(inside))
        def _():
            merged[t * KB : (t + 1) * KB] = jnp.zeros((KB,) + merged.shape[1:], jnp.bfloat16)

        groups = [a for a in range(owned // KB) if 0 <= t - 1 - a < OFFSETS // KB]

        def correlate(n, _):
            group = groups[0] + n // KB
            i = groups[0] * KB + n
            kb = t - 1 - group
            own = merged[i]
            other = merged[pl.ds(i + KB * kb, KB)]
            own_re, own_im = own[None, :, :half], own[None, :, half:]
            other_re, other_im = other[:, :, :half], other[:, :, half:]
            re = own_re * other_re + own_im * other_im
            im = own_re * other_im - own_im * other_re
            both = jnp.concatenate([re, im], axis=2).reshape(KB * span, 2 * half)
            total = jnp.dot(sum_rows, both, preferred_element_type=jnp.float32)
            total = jnp.where(real_row, total[:, :half], total[:, half:])
            rows = pl.ds(pl.multiple_of(2 * KB * kb, 2 * KB), 2 * KB)
            out[i, rows, :] = (total * inv[i, rows, :]).astype(jnp.bfloat16)
            return 0

        if groups:
            lax.fori_loop(0, len(groups) * KB, correlate, 0, unroll=16)

    def drain(b, _):
        for w in range(n_seg + 1):
            for h in range(n_freq):
                remote, local, mine, other = descriptor(b, w, h)
                pl.when(other)(remote.wait_send)
        if half_way < per_granule:
            for h in range(n_freq):
                copy, used = detour(b, h)
                pl.when(used)(copy.wait_send)
        return 0

    lax.fori_loop(0, chunks, drain, 0)
    for slot in range(per_granule - half_way):
        copy, used = onward(slot)
        pl.when(used)(copy.wait_send)
    for part in range(per_granule):
        for sx in range(n_seg):
            pl.when(along_used(sx, part))(along(sx, part).wait_send)
            for w in range(1, n_seg + 1):
                for tx in range(n_seg):
                    pl.when(hub_target(sx, w, tx))(across(sx, w, tx, part).wait_send)


def shards(samples, live):
    ch_dev, segs, length = samples.shape
    n_chan, n_seg, n_freq = (lax.axis_size(a) for a in ("chan", "seg", "freq"))
    owned = ch_dev // n_seg
    half = BINS // n_freq
    core_ch = ch_dev // n_freq
    chunks = core_ch // CHUNK_CH
    chunk_rows = CHUNK_CH * segs
    quarter = length // QUARTERS
    window = (n_seg + 1) * owned
    result = pl.pallas_call(
        functools.partial(kernel, n_chan, n_seg, n_freq),
        out_shape=jax.ShapeDtypeStruct((owned, 2 * OFFSETS, half), jnp.bfloat16),
        in_specs=[pl.BlockSpec(memory_space=pltpu.HBM)] * 2,
        out_specs=pl.BlockSpec(memory_space=pltpu.VMEM),
        scratch_shapes=[
            pltpu.VMEM(live.shape[::-1], jnp.int32),
            pltpu.VMEM(live.shape, jnp.float32),
            pltpu.VMEM((chunks, QUARTERS * chunk_rows, quarter), jnp.bfloat16),
            pltpu.VMEM((quarter, 2 * BINS), jnp.bfloat16),
            pltpu.VMEM((2, quarter // FINE, BINS), jnp.float32),
            pltpu.VMEM((n_freq, core_ch * segs, 2 * half), jnp.bfloat16),
            pltpu.VMEM((n_seg, n_seg + 1, owned * segs, 2 * half), jnp.bfloat16),
            pltpu.VMEM((window, n_seg * segs, 2 * half), jnp.bfloat16),
            pltpu.VMEM((window, n_seg * segs), jnp.float32),
            pltpu.VMEM((owned, 2 * OFFSETS, half), jnp.float32),
            pltpu.SemaphoreType.DMA,
            pltpu.SemaphoreType.DMA((chunks, QUARTERS)),
            pltpu.SemaphoreType.DMA((chunks, n_seg + 1, n_freq)),
            pltpu.SemaphoreType.DMA((n_seg, n_seg + 1, owned // CHUNK_CH)),
            pltpu.SemaphoreType.DMA((n_seg, owned // CHUNK_CH)),
            pltpu.SemaphoreType.DMA((n_seg, n_seg, n_seg, owned // CHUNK_CH)),
            pltpu.VMEM((owned // CHUNK_CH, chunk_rows, 2 * half), jnp.bfloat16),
            pltpu.SemaphoreType.DMA((owned // CHUNK_CH,)),
            pltpu.SemaphoreType.DMA((owned // CHUNK_CH,)),
        ],
        compiler_params=pltpu.CompilerParams(
            collective_id=0, has_side_effects=True, vmem_limit_bytes=48 * 1024 * 1024
        ),
    )(samples.reshape(ch_dev * segs, length), live.T)
    return result.reshape(owned, OFFSETS, 2, half)


def solution(mesh):
    return jax.shard_map(
        shards,
        mesh=mesh,
        in_specs=(P(("cable", "chan"), "seg", None), P("cable", None)),
        out_specs=P(("cable", "chan", "seg"), None, None, "freq"),
        check_vma=False,
    )
```
